256 devices in a mesh: section: 64 (over y_hi, x, z), dp: 4 (over y_lo, core).
Axes of the slice: x: 4, y: 4 (y_hi: 2, y_lo: 2; y = y_hi * 2 + y_lo), z: 8, core: 2. Of those that a mesh axis runs over, the one named last changes fastest.
Arguments:
- states: bfloat16 [64, 16, 32, 2688], P('section', None, 'dp'), may hold values from -6 to 6
- inject: bfloat16 [16, 32, 2688], P(None, 'dp'), may hold values from -6 to 6
- final_cotangent: bfloat16 [16, 32, 2688], P(None, 'dp'), may hold values from -6 to 6
- weight: bfloat16 [2688, 2688], P('dp'), may hold values from -0.125 to 0.125
- norm_gain: float32 [2688], replicated, may hold values from 0.1 to 1.9
Outputs:
- d_inject: float32 [16, 32, 2688], P(None, 'dp', 'section')
- d_weight: float32 [2688, 2688], P('section', 'dp')
- d_gain: float32 [2688], replicated
The draws below stay inside these ranges and needn't reach their ends.
All inputs are finite; a program needn't handle non-finite values.
Results may differ from the reference program's by a relative error of at most 0.018.
Values may be sent and summed in bfloat16 or wider, within the bound.
No kernel may reach another device: no remote copies, remote signals or barrier semaphores. Data moves between devices by JAX's collectives and lax.ppermute only.
A program may use at most 128 MiB of HBM per device.

```python
import math
import jax
import jax.numpy as jnp
from jax import lax

D = 2688
MICRO = 16
ITERS = 64
TOKENS = 32


def steps_of(key, dims, split, smallest, high):
    level, own = 1.0, jax.random.fold_in(key, 6)
    for dim, shards_of in split:
        heights = jnp.exp(jax.random.uniform(jax.random.fold_in(own, dim), (shards_of,), jnp.float32, smallest / len(split), high / len(split)))
        level = level * jnp.repeat(heights, dims[dim] // shards_of).reshape([-1 if axis == dim else 1 for axis in range(len(dims))])
    return level


def bell_draw(key, shape, width, bound, shards=(), kind=jnp.bfloat16):
    entries = width * jax.random.normal(key, shape, jnp.float32)
    if shards:
        entries = entries * steps_of(key, shape, shards, -0.22, 0.18)
    return jnp.clip(entries, -bound, bound).astype(kind)


def setup_inputs(seed: int = 0) -> dict:
    arg_keys = jax.random.split(jax.random.key(seed), 6)
    return {
        "states": bell_draw(arg_keys[0], (ITERS, MICRO, TOKENS, D), 1.0, 6.0, ((0, 64), (2, 4))),
        "inject": bell_draw(arg_keys[1], (MICRO, TOKENS, D), 1.0, 6.0, ((1, 4),)),
        "final_cotangent": bell_draw(arg_keys[2], (MICRO, TOKENS, D), 1.0, 6.0, ((1, 4),)),
        "weight": bell_draw(arg_keys[3], (D, D), D ** -0.5, 0.125, ((0, 4),)),
        "norm_gain": jnp.clip(1.0 + 0.18 * jax.random.normal(arg_keys[4], (D,), jnp.float32), 0.1, 1.9),
    }


EPSILON = 1e-06

def reference(states, inject, final_cotangent, weight, norm_gain):
    branch_scale = 1.0 / math.sqrt(ITERS)
    inject_wide = inject.astype(jnp.float32)
    model_width = weight.shape[0]

    def backward_step(state_carry, saved):
        upstream, gain_grad, weight_grad, inject_grad = state_carry
        mixed_input = saved.astype(jnp.float32) + inject_wide
        inverse_rms = lax.rsqrt(lax.optimization_barrier(jnp.mean(mixed_input * mixed_input, axis=-1, keepdims=True)) + EPSILON)
        normed = (mixed_input * inverse_rms * norm_gain).astype(jnp.bfloat16)
        flat_normed = normed.reshape(-1, model_width)
        hidden = jnp.dot(flat_normed, weight, preferred_element_type=jnp.float32).reshape(mixed_input.shape)
        sigmoid_h = jax.nn.sigmoid(hidden)
        upstream_wide = upstream.astype(jnp.float32)
        hidden_grad = (upstream_wide * sigmoid_h * (1.0 + hidden * (1.0 - sigmoid_h)) * branch_scale).astype(jnp.bfloat16)
        flat_grad = hidden_grad.reshape(-1, model_width)
        normed_grad = jnp.dot(flat_grad, weight.T, preferred_element_type=jnp.float32).reshape(mixed_input.shape)
        scaled_grad = normed_grad * norm_gain
        input_grad = inverse_rms * (scaled_grad - mixed_input * inverse_rms * inverse_rms * lax.optimization_barrier(jnp.mean(scaled_grad * mixed_input, axis=-1, keepdims=True)))
        gain_grad = gain_grad + lax.optimization_barrier(jnp.sum(normed_grad * mixed_input * inverse_rms, axis=(0, 1)))
        weight_grad = weight_grad + jnp.dot(flat_normed.T, flat_grad, preferred_element_type=jnp.float32)
        inject_grad = inject_grad + input_grad
        passed = (upstream_wide + input_grad).astype(jnp.bfloat16)
        return ((passed, gain_grad, weight_grad, inject_grad), None)
    initial = (final_cotangent, jnp.zeros((model_width,), jnp.float32), jnp.zeros((model_width, model_width), jnp.float32), jnp.zeros(inject.shape, jnp.float32))
    final_carry, unused = lax.scan(backward_step, initial, states, reverse=True)
    return (final_carry[3], final_carry[2], final_carry[1])
```

```python
import functools
import math

import jax
import jax.numpy as jnp
from jax import lax
from jax.experimental import pallas as pl
from jax.experimental.pallas import tpu as pltpu
from jax.sharding import PartitionSpec as P

EPSILON = 1e-06
TOLERANCE = 2.0**-10
LANES = 128
AXES = ("section", "dp")
Y_HI, X, Z, Y_LO, CORE = 2, 4, 8, 2, 2


def flat(y, x, z, core):
    return (((y // Y_LO) * X + x) * Z + z) * 4 + (y % Y_LO) * CORE + core


PLACES = [
    (y, x, z, core)
    for y in range(Y_HI * Y_LO)
    for x in range(X)
    for z in range(Z)
    for core in range(CORE)
]


def move(value, target):
    return lax.ppermute(value, AXES, [(flat(*place), flat(*target(*place))) for place in PLACES])


def other_core(y, x, z, core):
    return (y, x, z, 1 - core)


def y_up(y, x, z, core):
    return ((y + 1) % (Y_HI * Y_LO), x, z, core)


def y_down(y, x, z, core):
    return ((y - 1) % (Y_HI * Y_LO), x, z, core)


XD_GROUPS = [
    [flat(yh * Y_LO + d // CORE, x, z, d % CORE) for x in range(X) for d in range(4)]
    for yh in range(Y_HI)
    for z in range(Z)
]
YZ_GROUPS = [
    [flat(yh * Y_LO + d // CORE, x, z, d % CORE) for yh in range(Y_HI) for z in range(Z)]
    for x in range(X)
    for d in range(4)
]


def gather_weight(weight):
    rows = weight.shape[0]
    half = rows // 2
    cuts = [0, half // 32 * 16, half]
    pieces, offsets = [weight], [(0, 0, rows)]
    pieces.append(move(weight, other_core))
    offsets.append((1, 0, rows))
    far = []
    for low, high in zip(cuts[:-1], cuts[1:]):
        far.append((move(weight[low:high], y_up), low))
        far.append((move(weight[half + low : half + high], y_down), half + low))
    for piece, low in far:
        pieces += [piece, move(piece, other_core)]
        offsets += [(2, low, piece.shape[0]), (3, low, piece.shape[0])]
    return pieces, tuple(offsets)

def solve_kernel(offsets, dim, rows, max_sweeps, tolerance, shard_ref, *refs):
    pieces = refs[:len(offsets)]
    a_ref, x_ref, q_ref, gain_ref, fc_ref = refs[len(offsets):len(offsets)+5]
    g_ref, dinj_ref, dgain_ref = refs[len(offsets)+5:len(offsets)+8]
    w, wt, slope, t, p, v, sems = refs[len(offsets)+8:]
    shard = shard_ref[0]
    shard_rows = dim // 4
    copies=[]
    for n,((flip, off, cnt), piece) in enumerate(zip(offsets, pieces)):
        at = pl.multiple_of(lax.bitwise_xor(shard, flip) * shard_rows + off, 16)
        copy = pltpu.make_async_copy(piece, w.at[pl.ds(at, cnt)], sems.at[n])
        copy.start(); copies.append(copy)
    for copy in copies: copy.wait()
    groups = rows // 8
    wide = 384 if dim % 384 == 0 else 128
    scale = (1.0/max_sweeps) ** 0.5
    for j in range(0, dim, wide):
        cols = slice(j, j+wide)
        h = jnp.dot(a_ref[...], w[:, cols], preferred_element_type=jnp.float32)
        s = jax.nn.sigmoid(h)
        sl = s*(1.0+h*(1.0-s))*scale
        slope[:, cols] = sl
        fc = fc_ref[:, cols]
        v[:, cols] = (sl*jnp.concatenate([fc]*groups,0)).astype(jnp.bfloat16)
        p[:, cols] = jnp.zeros_like(sl)
    for j in range(0, dim, LANES):
        wt[j:j+LANES, :] = w[:, j:j+LANES].T
    sub = lax.broadcasted_iota(jnp.int32, (8, LANES), 0)
    def sweep(carry):
        count, _ = carry
        macc = jnp.zeros((rows, LANES), jnp.float32)
        for j in range(0, dim, wide):
            cols = slice(j, j+wide)
            u = jnp.dot(v[...], wt[:, cols], preferred_element_type=jnp.float32)
            tt = u * gain_ref[0:1, cols]
            t[:, cols] = tt
            tx = tt * x_ref[:, cols]
            for k in range(0, wide, LANES):
                macc = macc + tx[:, k:k+LANES]
        q = q_ref[...]
        kap = q*q*q*(jnp.sum(macc, axis=1, keepdims=True) * (1.0/dim))
        dacc = jnp.zeros((8, LANES), jnp.float32)
        cacc = jnp.zeros((8, LANES), jnp.float32)
        for j in range(0, dim, LANES):
            cols = slice(j, j+LANES)
            run = None
            sums = [None]*groups
            for b in range(groups-1, -1, -1):
                rs = slice(8*b, 8*b+8)
                pn = q[rs]*t[rs, cols] - kap[rs]*x_ref[rs, cols]
                d = pn - p[rs, cols]
                p[rs, cols] = pn
                dacc = dacc + d*d
                run = pn if run is None else run + pn
                sums[b] = run
            dinj_ref[:, cols] = run
            base = fc_ref[:, cols]
            for k in (2, 4, 6):
                base = base + jnp.where(sub < 8-k, pltpu.roll(run, 8-k, 0), 0.0)
            for b in range(groups):
                rs = slice(8*b, 8*b+8)
                c = base if b == groups-1 else base + sums[b+1]
                cacc = cacc + c*c
                v[rs, cols] = (c*slope[rs, cols]).astype(jnp.bfloat16)
        dn = jnp.sum(dacc, axis=1, keepdims=True)
        cn = jnp.sum(cacc, axis=1, keepdims=True)
        open_rows = jnp.sum(jnp.where(dn <= cn*(tolerance*tolerance), 0.0, 1.0))
        return count+1, open_rows
    last, _ = lax.while_loop(lambda cr: jnp.logical_and(cr[0] < max_sweeps, cr[1] > 0.0), sweep, (jnp.int32(0), jnp.float32(1)))
    for j in range(0, dim, LANES):
        cols = slice(j, j+LANES)
        acc = jnp.zeros((8, LANES), jnp.float32)
        for b in range(groups):
            rs = slice(8*b, 8*b+8)
            acc = acc + q_ref[rs]*t[rs, cols]*x_ref[rs, cols]
        dgain_ref[:, cols] = acc / gain_ref[0:1, cols]
    for k in range(4):
        g_ref[k] = v[:, k*shard_rows:(k+1)*shard_rows]


def solve(shard, pieces, offsets, a, x, q, gain, fc, tolerance):
    rows, dim = a.shape
    n = len(pieces)
    vm = pl.BlockSpec(memory_space=pltpu.VMEM)
    f32 = jnp.float32
    return pl.pallas_call(
        functools.partial(solve_kernel, offsets, dim, rows, 64, tolerance),
        out_shape=(jax.ShapeDtypeStruct((4, rows, dim//4), jnp.bfloat16), jax.ShapeDtypeStruct((8, dim), f32), jax.ShapeDtypeStruct((8, dim), f32)),
        in_specs=[pl.BlockSpec(memory_space=pltpu.SMEM)]+[pl.BlockSpec(memory_space=pl.ANY)]*n+[vm]*5,
        out_specs=(vm,)*3,
        scratch_shapes=[pltpu.VMEM((dim,dim),jnp.bfloat16)]*2+[pltpu.VMEM((rows,dim),f32)]*3+[pltpu.VMEM((rows,dim),jnp.bfloat16), pltpu.SemaphoreType.DMA((n,))],
        compiler_params=pltpu.CompilerParams(vmem_limit_bytes=58*2**20),
    )(shard, *pieces, a, x, q, gain, fc)


def per_device(states, inject, final_cotangent, weight, norm_gain):
    micro_count, row_count, dim = inject.shape
    sections = lax.axis_size("section")
    section, shard = lax.axis_index("section"), lax.axis_index("dp")
    own = micro_count * row_count // sections
    segments, groups = 4, sections // 4
    f32, bf16 = jnp.float32, jnp.bfloat16
    pieces, offsets = gather_weight(weight)

    mine = lax.all_to_all(states[0].reshape(sections, own, dim), "section", 0, 0)
    mine = mine.reshape(segments, groups, own, dim).transpose(1, 0, 2, 3)
    inject_own = lax.dynamic_index_in_dim(inject.reshape(sections, own, dim), section, 0, keepdims=False)
    final_own = lax.dynamic_index_in_dim(final_cotangent.reshape(sections, own, dim), section, 0, keepdims=False)
    x = (mine.astype(f32) + inject_own.astype(f32)).reshape(-1, dim)
    rows = x.shape[0]
    q = lax.rsqrt(jnp.mean(x * x, axis=-1, keepdims=True) + EPSILON)
    a = (x * q * norm_gain).astype(bf16)

    a_cut = a.reshape(rows, Y_HI, X, dim // 8).transpose(2, 0, 1, 3).reshape(X, 1, rows, dim // 4)
    a_cut = jnp.broadcast_to(a_cut, (X, 4, rows, dim // 4)).reshape(16, rows, dim // 4)
    a_all = lax.all_to_all(a_cut, AXES, 0, 0, axis_index_groups=XD_GROUPS)

    g, d_inject, d_gain = solve(
        shard.astype(jnp.int32).reshape(1),
        pieces,
        offsets,
        a,
        x,
        jnp.broadcast_to(q, (rows, LANES)),
        jnp.broadcast_to(norm_gain, (8, dim)),
        jnp.tile(final_own.astype(f32), (segments, 1)),
        TOLERANCE,
    )
    d_inject = jnp.sum(d_inject.reshape(segments, own, dim), axis=0)
    d_gain = jnp.sum(d_gain, axis=0)

    d_inject_cut = d_inject.astype(bf16).reshape(own, Y_HI, X, dim // 8).transpose(2, 0, 1, 3).reshape(X, own, dim // 4)
    d_gain_cut = d_gain.astype(bf16).reshape(4, dim // 4)
    pad = jnp.zeros((X, 4, 16 - own - 4, dim // 4), bf16)
    out = jnp.concatenate(
        [
            jnp.broadcast_to(g[None], (X, 4, rows, dim // 4)),
            jnp.broadcast_to(d_inject_cut[:, None], (X, 4, own, dim // 4)),
            jnp.broadcast_to(d_gain_cut[None, None], (X, 4, 4, dim // 4)),
            pad,
        ],
        axis=2,
    ).reshape(16, rows + 16, dim // 4)
    got = lax.all_to_all(out, AXES, 0, 0, axis_index_groups=XD_GROUPS)
    block = lax.dot_general(
        a_all, got[:, :rows], (((0, 1), (0, 1)), ((), ())), preferred_element_type=f32
    )
    gain_sum = jnp.sum(got[:, rows + own : rows + own + 4].astype(f32), axis=0)
    inject_got = lax.dynamic_index_in_dim(got.reshape(X, 4, rows + 16, dim // 4), shard, 1, keepdims=False)
    inject_got = inject_got[:, rows : rows + own].reshape(X * own, 16, dim // 64).transpose(1, 0, 2)
    inject_row = jnp.pad(inject_got.reshape(16, 1, -1), ((0, 0), (0, 0), (0, dim // 4 - X * own * (dim // 64))))

    part = dim // 64
    out = jnp.concatenate(
        [
            block.reshape(16, part, dim // 4).astype(bf16),
            inject_row,
            jnp.broadcast_to(gain_sum.astype(bf16)[None], (16, 4, dim // 4)),
            jnp.zeros((16, 48 - part - 5, dim // 4), bf16),
        ],
        axis=1,
    )
    got = lax.all_to_all(out, AXES, 0, 0, axis_index_groups=YZ_GROUPS)
    total = jnp.sum(got.astype(f32), axis=0)
    d_weight = total[:part]
    d_gain = total[part + 1 : part + 5].reshape(dim)
    d_inject = got[:, part, : X * own * part].reshape(Y_HI, Z, X, own, part).transpose(0, 2, 1, 3, 4)
    d_inject = d_inject.reshape(micro_count, row_count, part).astype(f32)
    return d_inject, d_weight, d_gain


def solution(mesh):
    in_specs = (
        P("section", None, "dp", None),
        P(None, "dp", None),
        P(None, "dp", None),
        P("dp", None),
        P(),
    )
    out_specs = (P(None, "dp", "section"), P("section", "dp"), P())
    return jax.shard_map(
        per_device, mesh=mesh, in_specs=in_specs, out_specs=out_specs, check_vma=False
    )
```

```python
import functools
import math

import jax
import jax.numpy as jnp
from jax import lax
from jax.experimental import pallas as pl
from jax.experimental.pallas import tpu as pltpu
from jax.sharding import PartitionSpec as P

EPSILON = 1e-06
TOLERANCE = 2.0**-10
LANES = 128
AXES = ("section", "dp")
Y_HI, X, Z, Y_LO, CORE = 2, 4, 8, 2, 2
f32, bf16 = jnp.float32, jnp.bfloat16


def own_tokens(ref, section, copies):
    block = ref[section // 4].astype(f32)
    pair = block[0:2]
    for k in range(1, 4):
        pair = jnp.where(section % 4 == k, block[2 * k : 2 * k + 2], pair)
    return jnp.concatenate([pair] * copies, axis=0)


def prepare_kernel(place_ref, states_ref, inject_ref, gain_ref, x_ref, a_ref, q_ref, *cut_refs):
    rows, dim = x_ref.shape
    section = place_ref[0]
    inject = own_tokens(inject_ref, section, 4)
    gain = gain_ref[...]
    groups = rows // 8

    def one(b, _):
        x = jnp.concatenate([states_ref[seg * groups + b].astype(f32) for seg in range(4)], axis=0) + inject
        q = lax.rsqrt(jnp.sum(x * x, axis=1, keepdims=True) * (1.0 / dim) + EPSILON)
        at = pl.ds(pl.multiple_of(b * 8, 8), 8)
        x_ref[at, :] = x
        q_ref[at, :] = jnp.broadcast_to(q, (8, LANES))
        return 0

    lax.fori_loop(0, groups, one, 0)
    a_ref[...] = (x_ref[...] * q_ref[:, 0:1] * gain).astype(bf16)
    eighth = dim // 8
    place = (section // Z) % X
    for cut_ref in cut_refs:
        cut_ref[:, 2 * eighth :] = jnp.zeros((rows, cut_ref.shape[1] - 2 * eighth), bf16)
    for own in range(X):

        @pl.when(place == own)
        def _():
            for step in range(X):
                k = (own + step) % X
                cut_refs[step][:, 0:eighth] = a_ref[:, k * eighth : (k + 1) * eighth]
                cut_refs[step][:, eighth : 2 * eighth] = a_ref[:, dim // 2 + k * eighth : dim // 2 + (k + 1) * eighth]


def prepare(place, states, inject, gain):
    rows, dim = states.shape[0] * states.shape[1], states.shape[2]
    vm = pl.BlockSpec(memory_space=pltpu.VMEM)
    return pl.pallas_call(
        prepare_kernel,
        out_shape=(
            jax.ShapeDtypeStruct((rows, dim), f32),
            jax.ShapeDtypeStruct((rows, dim), bf16),
            jax.ShapeDtypeStruct((rows, LANES), f32),
        )
        + (jax.ShapeDtypeStruct((rows, pl.cdiv(dim // 4, LANES) * LANES), bf16),) * X,
        in_specs=[pl.BlockSpec(memory_space=pltpu.SMEM)] + [vm] * 3,
        out_specs=(vm,) * (3 + X),
        compiler_params=pltpu.CompilerParams(vmem_limit_bytes=32 * 2**20),
        cost_estimate=pl.CostEstimate(flops=20 * 10**9, bytes_accessed=4 * 2**20, transcendentals=0),
    )(place, states, inject, gain)


def solve_kernel(offsets, max_sweeps, tolerance, place_ref, *refs):
    count = len(offsets)
    pieces = refs[:count]
    a_ref, x_ref, q_ref, gain_ref, final_ref = refs[count : count + 5]
    outs = refs[count + 5 : count + 9]
    w, wt, slope, t, p, v, inject_sum, gain_sum, final, sems = refs[count + 9 :]
    rows, dim = x_ref.shape
    section, shard = place_ref[0], place_ref[1]
    small, eighth, groups = dim // 4, dim // 8, rows // 8
    wide = 384 if dim % 384 == 0 else LANES

    copies = []
    for n, ((flip, start, length), piece) in enumerate(zip(offsets, pieces)):
        at = pl.multiple_of(lax.bitwise_xor(shard, flip) * small + start, 16)
        copies.append(pltpu.make_async_copy(piece, w.at[pl.ds(at, length)], sems.at[n]))
        copies[-1].start()
    final[...] = own_tokens(final_ref, section, 4)
    p[...] = jnp.zeros_like(p)
    for copy in copies:
        copy.wait()

    def start(n, _):
        cols = pl.ds(pl.multiple_of(n * wide, LANES), wide)
        h = jnp.dot(a_ref[...], w[:, cols], preferred_element_type=f32)
        s = jax.nn.sigmoid(h)
        sl = s * (1.0 + h * (1.0 - s)) * (1.0 / math.sqrt(max_sweeps))
        slope[:, cols] = sl
        v[:, cols] = (sl * jnp.concatenate([final[:, cols]] * groups, axis=0)).astype(bf16)
        for k in range(0, wide, LANES):
            wt[pl.ds(pl.multiple_of(n * wide + k, LANES), LANES), :] = w[:, pl.ds(pl.multiple_of(n * wide + k, LANES), LANES)].T
        return 0

    lax.fori_loop(0, dim // wide, start, 0)
    sub = lax.broadcasted_iota(jnp.int32, (8, LANES), 0)

    def sweep(carry):
        done, _ = carry
        acc = jnp.zeros((rows, LANES), f32)
        for j in range(0, dim, wide):
            cols = slice(j, j + wide)
            u = jnp.dot(v[...], wt[:, cols], preferred_element_type=f32)
            scaled = u * gain_ref[0:1, cols]
            t[:, cols] = scaled
            scaled = scaled * x_ref[:, cols]
            for k in range(0, wide, LANES):
                acc = acc + scaled[:, k : k + LANES]
        q = q_ref[...]
        kappa = q * q * q * (jnp.sum(acc, axis=1, keepdims=True) * (1.0 / dim))

        def columns(n, sums):
            moved, size = sums
            cols = pl.ds(pl.multiple_of(n * LANES, LANES), LANES)
            run, tails = None, [None] * groups
            for b in range(groups - 1, -1, -1):
                at = slice(8 * b, 8 * b + 8)
                new = q[at] * t[at, cols] - kappa[at] * x_ref[at, cols]
                step = new - p[at, cols]
                p[at, cols] = new
                moved = moved + step * step
                run = new if run is None else run + new
                tails[b] = run
            inject_sum[:, cols] = run
            base = final[:, cols]
            for k in (2, 4, 6):
                base = base + jnp.where(sub < 8 - k, pltpu.roll(run, 8 - k, 0), 0.0)
            for b in range(groups):
                at = slice(8 * b, 8 * b + 8)
                c = base if b == groups - 1 else base + tails[b + 1]
                size = size + c * c
                v[at, cols] = (c * slope[at, cols]).astype(bf16)
            return moved, size

        zero = jnp.zeros((8, LANES), f32)
        moved, size = lax.fori_loop(0, dim // LANES, columns, (zero, zero), unroll=3)
        moved = jnp.sum(moved, axis=1, keepdims=True)
        size = jnp.sum(size, axis=1, keepdims=True)
        still = jnp.sum(jnp.where(moved <= size * (tolerance * tolerance), 0.0, 1.0))
        return done + 1, still

    lax.while_loop(
        lambda carry: jnp.logical_and(carry[0] < max_sweeps, carry[1] > 0.0),
        sweep,
        (jnp.int32(0), jnp.float32(1)),
    )

    def finish(n, _):
        cols = pl.ds(pl.multiple_of(n * LANES, LANES), LANES)
        acc = jnp.zeros((8, LANES), f32)
        for b in range(groups):
            at = slice(8 * b, 8 * b + 8)
            acc = acc + q_ref[at] * t[at, cols] * x_ref[at, cols]
        gain_sum[:, cols] = acc / gain_ref[0:1, cols]
        return 0

    lax.fori_loop(0, dim // LANES, finish, 0)
    wide_sub = lax.broadcasted_iota(jnp.int32, (8, small), 0)
    gain_rows = jnp.zeros((8, small), f32)
    total = jnp.sum(gain_sum[...], axis=0, keepdims=True)
    for k in range(4):
        gain_rows = jnp.where(wide_sub == k, total[:, k * small : (k + 1) * small], gain_rows)
    inject_rows = jnp.zeros((8, small), f32)
    total = inject_sum[...]
    total = total + pltpu.roll(total, 4, 0)
    total = total + pltpu.roll(total, 2, 0)
    for k in range(X):
        part = jnp.concatenate(
            [total[:, k * eighth : (k + 1) * eighth], total[:, dim // 2 + k * eighth : dim // 2 + (k + 1) * eighth]],
            axis=1,
        )
        inject_rows = jnp.where(wide_sub // 2 == k, part, inject_rows)
    extra = jnp.concatenate([inject_rows, gain_rows], axis=0).astype(bf16)
    for own in range(4):

        @pl.when(shard == own)
        def _():
            for flip in range(4):
                block = own ^ flip
                outs[flip][0:rows] = v[:, block * small : (block + 1) * small]

    for flip in range(4):
        outs[flip][rows : rows + 16] = extra


def solve(place, pieces, offsets, a, x, q, gain, final, tolerance):
    rows, dim = x.shape
    n = len(pieces)
    vm = pl.BlockSpec(memory_space=pltpu.VMEM)
    return pl.pallas_call(
        functools.partial(solve_kernel, offsets, 64, tolerance),
        out_shape=(jax.ShapeDtypeStruct((rows + 16, dim // 4), bf16),) * 4,
        in_specs=[pl.BlockSpec(memory_space=pltpu.SMEM)] + [pl.BlockSpec(memory_space=pl.ANY)] * n + [vm] * 5,
        out_specs=(vm,) * 4,
        scratch_shapes=[pltpu.VMEM((dim, dim), bf16)] * 2
        + [pltpu.VMEM((rows, dim), f32)] * 3
        + [pltpu.VMEM((rows, dim), bf16)]
        + [pltpu.VMEM((8, dim), f32)] * 3
        + [pltpu.SemaphoreType.DMA((n,))],
        compiler_params=pltpu.CompilerParams(vmem_limit_bytes=56 * 2**20),
        cost_estimate=pl.CostEstimate(flops=4 * 10**10, bytes_accessed=16 * 2**20, transcendentals=0),
    )(place, *pieces, a, x, q, gain, final)


def block_kernel(rows, dim, place_ref, *refs):
    a_refs, own_refs, far_refs = refs[:4], refs[4:8], refs[8:12]
    out_ref, a, g, sems = refs[12:]
    small, part = dim // 4, dim // 64
    tall = rows + 16
    copies = [pltpu.make_async_copy(a_refs[flip], a.at[flip], sems.at[flip]) for flip in range(4)]
    for step in range(X):
        copies.append(pltpu.make_async_copy(own_refs[step], g.at[pl.ds(step * tall, tall)], sems.at[4 + step]))
        copies.append(pltpu.make_async_copy(far_refs[step], g.at[pl.ds((4 + 3 * step) * tall, 3 * tall)], sems.at[8 + step]))
    for copy in copies:
        copy.start()
    for copy in copies:
        copy.wait()

    def slot(flip, step):
        return tall * (step if flip == 0 else 3 + 3 * step + flip)

    places = [(flip, step) for flip in range(4) for step in range(X)]
    left = jnp.concatenate([a[flip, step * rows : (step + 1) * rows] for flip, step in places], axis=0)
    right = jnp.concatenate([g[slot(flip, step) : slot(flip, step) + rows] for flip, step in places], axis=0)
    block = lax.dot_general(left, right, (((0,), (0,)), ((), ())), preferred_element_type=f32)
    gain = jnp.zeros((8, small), f32)
    injects = []
    for flip, step in places:
        extra = g[slot(flip, step) + rows : slot(flip, step) + tall].astype(f32)
        gain = gain + extra[8:16]
        if flip == 0:
            own = extra[0:2]
            for k in range(1, X):
                own = jnp.where((place_ref[0] // Z) % X == k, extra[2 * k : 2 * k + 2], own)
            injects.append(own)
    inject = jnp.concatenate(injects, axis=0)
    for k in range(16):
        line = jnp.concatenate(
            [inject[n : n + 1, k * part : (k + 1) * part] for n in range(8)] + [jnp.zeros((1, small - 8 * part), f32)],
            axis=1,
        )
        out_ref[k] = jnp.concatenate([block[k * part : (k + 1) * part], line, gain[0:5]], axis=0).astype(bf16)


def block_sum(place, a_parts, own_parts, far_parts):
    rows, small = a_parts[0].shape[0] // X, own_parts[0].shape[1]
    hold = pl.BlockSpec(memory_space=pl.ANY)
    return pl.pallas_call(
        functools.partial(block_kernel, rows, 4 * small),
        out_shape=jax.ShapeDtypeStruct((16, 48, small), bf16),
        in_specs=[pl.BlockSpec(memory_space=pltpu.SMEM)] + [hold] * 12,
        out_specs=pl.BlockSpec(memory_space=pltpu.VMEM),
        scratch_shapes=[
            pltpu.VMEM((4,) + a_parts[0].shape, bf16),
            pltpu.VMEM((16 * (rows + 16), small), bf16),
            pltpu.SemaphoreType.DMA((12,)),
        ],
        compiler_params=pltpu.CompilerParams(vmem_limit_bytes=48 * 2**20),
    )(place, *a_parts, *own_parts, *far_parts)


def flat(y, x, z, core):
    return (((y // Y_LO) * X + x) * Z + z) * 4 + (y % Y_LO) * CORE + core


PLACES = [
    (y, x, z, core)
    for y in range(Y_HI * Y_LO)
    for x in range(X)
    for z in range(Z)
    for core in range(CORE)
]


def move(value, target):
    return lax.ppermute(value, AXES, [(flat(*place), flat(*target(*place))) for place in PLACES])


def y_move(value, steps):
    return move(value, lambda y, x, z, core: ((y + steps) % (Y_HI * Y_LO), x, z, core))


def x_move(value, steps):
    return move(value, lambda y, x, z, core: (y, (x + steps) % X, z, core))


def dp_move(value, flip):
    return move(value, lambda y, x, z, core: (y ^ (flip // CORE), x, z, core ^ (flip % CORE)))


YZ_GROUPS = [
    [flat(yh * Y_LO + d // CORE, x, z, d % CORE) for yh in range(Y_HI) for z in range(Z)]
    for x in range(X)
    for d in range(4)
]


def gather_weight(weight):
    half = weight.shape[0] // 2
    pieces, offsets = [weight, dp_move(weight, 1)], [(0, 0, 2 * half), (1, 0, 2 * half)]
    source = weight
    cuts = (0, 128, 240, 336)
    for low, high in zip(cuts[:-1], cuts[1:]):
        up, down = y_move(source[low:high], 1), y_move(source[half + low : half + high], -1)
        source, up, down = lax.optimization_barrier((source, up, down))
        for piece, start in ((up, low), (down, half + low)):
            pieces += [piece, dp_move(piece, 1)]
            offsets += [(2, start, high - low), (3, start, high - low)]
    return pieces, tuple(offsets)


def per_device(states, inject, final_cotangent, weight, norm_gain):
    micro_count, row_count, dim = inject.shape
    sections = lax.axis_size("section")
    section, shard = lax.axis_index("section"), lax.axis_index("dp")
    own = micro_count * row_count // sections
    place = jnp.stack([section, shard]).astype(jnp.int32)
    gain = norm_gain.reshape(1, dim)
    pieces, offsets = gather_weight(weight)

    mine = lax.all_to_all(states[0].reshape(sections, own, dim), "section", 0, 0)
    x, a, q, *a_cut = prepare(place, mine, inject, gain)

    a_ring = jnp.concatenate([a_cut[0]] + [x_move(a_cut[step], step) for step in range(1, X)])
    a_parts = [a_ring] + [dp_move(a_ring, flip) for flip in (1, 2, 3)]

    g_parts = solve(place, pieces, offsets, a, x, q, gain, final_cotangent, TOLERANCE)

    (a_parts, g_parts) = lax.optimization_barrier((a_parts, g_parts))
    far = jnp.concatenate([dp_move(g_parts[flip], flip) for flip in (1, 2, 3)])
    own_parts = [g_parts[0]] + [x_move(g_parts[0], step) for step in range(1, X)]
    far, own_parts = lax.optimization_barrier((far, own_parts))
    far_parts = [far] + [x_move(far, step) for step in range(1, X)]
    out = block_sum(place, a_parts, own_parts, far_parts)

    got = lax.all_to_all(out, AXES, 0, 0, axis_index_groups=YZ_GROUPS)
    part = dim // 64
    total = jnp.sum(got.astype(f32), axis=0)
    d_weight = total[:part]
    d_gain = total[part + 1 : part + 5].reshape(dim)
    d_inject = got[:, part, : X * own * part].reshape(Y_HI, Z, X, own, part)
    d_inject = jnp.roll(d_inject[:, :, ::-1], (section // Z) % X + 1, axis=2).transpose(0, 2, 1, 3, 4)
    d_inject = d_inject.reshape(micro_count, row_count, part).astype(f32)
    return d_inject, d_weight, d_gain


def solution(mesh):
    in_specs = (
        P("section", None, "dp", None),
        P(None, "dp", None),
        P(None, "dp", None),
        P("dp", None),
        P(),
    )
    out_specs = (P(None, "dp", "section"), P("section", "dp"), P())
    return jax.shard_map(
        per_device, mesh=mesh, in_specs=in_specs, out_specs=out_specs, check_vma=False
    )
```

```python
import functools
import math

import jax
import jax.numpy as jnp
from jax import lax
from jax.experimental import pallas as pl
from jax.experimental.pallas import tpu as pltpu
from jax.sharding import PartitionSpec as P

EPSILON = 1e-06
TOLERANCE = 2.0**-10
LANES = 128
AXES = ("section", "dp")
Y_HI, X, Z, Y_LO, CORE = 2, 4, 8, 2, 2
LEFT, LEFT_GAIN = 384, 5
f32, bf16 = jnp.float32, jnp.bfloat16


def own_tokens(ref, section, copies):
    block = ref[section // 4].astype(f32)
    pair = block[0:2]
    for k in range(1, 4):
        pair = jnp.where(section % 4 == k, block[2 * k : 2 * k + 2], pair)
    return jnp.concatenate([pair] * copies, axis=0)


def prepare_kernel(place_ref, states_ref, inject_ref, gain_ref, x_ref, a_ref, q_ref, cut_ref, cuts, sems):
    rows, dim = x_ref.shape
    section = place_ref[0]
    inject = own_tokens(inject_ref, section, 4)
    gain = gain_ref[...]
    groups = rows // 8

    def one(b, _):
        x = jnp.concatenate([states_ref[seg * groups + b].astype(f32) for seg in range(4)], axis=0) + inject
        q = lax.rsqrt(jnp.sum(x * x, axis=1, keepdims=True) * (1.0 / dim) + EPSILON)
        at = pl.ds(pl.multiple_of(b * 8, 8), 8)
        x_ref[at, :] = x
        q_ref[at, :] = jnp.broadcast_to(q, (8, LANES))
        return 0

    lax.fori_loop(0, groups, one, 0)
    a_ref[...] = (x_ref[...] * q_ref[:, 0:1] * gain).astype(bf16)
    eighth = dim // 8
    copies = []
    for k in range(X):
        cut = jnp.concatenate(
            [
                a_ref[:, k * eighth : (k + 1) * eighth],
                a_ref[:, dim // 2 + k * eighth : dim // 2 + (k + 1) * eighth],
                jnp.zeros((rows, cuts.shape[2] - 2 * eighth), bf16),
            ],
            axis=1,
        )
        cuts[k] = cut
        copies += [pltpu.make_async_copy(cuts.at[k], cut_ref.at[n], sems.at[n]) for n in range(4 * k, 4 * k + 4)]
        for copy in copies[4 * k :]:
            copy.start()
    for copy in copies:
        copy.wait()


def prepare(place, states, inject, gain):
    rows, dim = states.shape[0] * states.shape[1], states.shape[2]
    vm = pl.BlockSpec(memory_space=pltpu.VMEM)
    return pl.pallas_call(
        prepare_kernel,
        out_shape=(
            jax.ShapeDtypeStruct((rows, dim), f32),
            jax.ShapeDtypeStruct((rows, dim), bf16),
            jax.ShapeDtypeStruct((rows, LANES), f32),
            jax.ShapeDtypeStruct((16, rows, pl.cdiv(dim // 4, LANES) * LANES), bf16),
        ),
        in_specs=[pl.BlockSpec(memory_space=pltpu.SMEM)] + [vm] * 3,
        out_specs=(vm,) * 3 + (pl.BlockSpec(memory_space=pltpu.HBM),),
        scratch_shapes=[
            pltpu.VMEM((X, rows, pl.cdiv(dim // 4, LANES) * LANES), bf16),
            pltpu.SemaphoreType.DMA((16,)),
        ],
        compiler_params=pltpu.CompilerParams(vmem_limit_bytes=32 * 2**20),
        cost_estimate=pl.CostEstimate(flops=60 * 10**9, bytes_accessed=4 * 2**20, transcendentals=0),
    )(place, states, inject, gain)


def solve_kernel(offsets, max_sweeps, tolerance, place_ref, *refs):
    count = len(offsets)
    pieces = refs[:count]
    a_ref, x_ref, q_ref, gain_ref, final_ref = refs[count : count + 5]
    outs = refs[count + 5 : count + 13]
    w, wt, slope, t, p, v, inject_sum, gain_sum, final, sems = refs[count + 13 :]
    rows, dim = x_ref.shape
    section, shard = place_ref[0], place_ref[1]
    small, eighth, groups = dim // 4, dim // 8, rows // 8
    wide = 384 if dim % 384 == 0 else LANES

    copies = []
    for n, ((flip, start, length), piece) in enumerate(zip(offsets, pieces)):
        at = pl.multiple_of(lax.bitwise_xor(shard, flip) * small + start, 16)
        copies.append(pltpu.make_async_copy(piece, w.at[pl.ds(at, length)], sems.at[n]))
        copies[-1].start()
    final[...] = own_tokens(final_ref, section, 4)
    p[...] = jnp.zeros_like(p)
    for copy in copies:
        copy.wait()

    def start(n, _):
        cols = pl.ds(pl.multiple_of(n * wide, LANES), wide)
        h = jnp.dot(a_ref[...], w[:, cols], preferred_element_type=f32)
        s = jax.nn.sigmoid(h)
        sl = s * (1.0 + h * (1.0 - s)) * (1.0 / math.sqrt(max_sweeps))
        slope[:, cols] = sl
        v[:, cols] = (sl * jnp.concatenate([final[:, cols]] * groups, axis=0)).astype(bf16)
        for k in range(0, wide, LANES):
            wt[pl.ds(pl.multiple_of(n * wide + k, LANES), LANES), :] = w[:, pl.ds(pl.multiple_of(n * wide + k, LANES), LANES)].T
        return 0

    lax.fori_loop(0, dim // wide, start, 0)
    sub = lax.broadcasted_iota(jnp.int32, (8, LANES), 0)

    def sweep(carry):
        done, _ = carry
        acc = jnp.zeros((rows, LANES), f32)
        for j in range(0, dim, wide):
            cols = slice(j, j + wide)
            u = jnp.dot(v[...], wt[:, cols], preferred_element_type=f32)
            scaled = u * gain_ref[0:1, cols]
            t[:, cols] = scaled
            scaled = scaled * x_ref[:, cols]
            for k in range(0, wide, LANES):
                acc = acc + scaled[:, k : k + LANES]
        q = q_ref[...]
        kappa = q * q * q * (jnp.sum(acc, axis=1, keepdims=True) * (1.0 / dim))

        def columns(n, sums):
            moved, size = sums
            cols = pl.ds(pl.multiple_of(n * LANES, LANES), LANES)
            run, tails = None, [None] * groups
            for b in range(groups - 1, -1, -1):
                at = slice(8 * b, 8 * b + 8)
                new = q[at] * t[at, cols] - kappa[at] * x_ref[at, cols]
                step = new - p[at, cols]
                p[at, cols] = new
                moved = moved + step * step
                run = new if run is None else run + new
                tails[b] = run
            inject_sum[:, cols] = run
            base = final[:, cols]
            for k in (2, 4, 6):
                base = base + jnp.where(sub < 8 - k, pltpu.roll(run, 8 - k, 0), 0.0)
            for b in range(groups):
                at = slice(8 * b, 8 * b + 8)
                c = base if b == groups - 1 else base + tails[b + 1]
                size = size + c * c
                v[at, cols] = (c * slope[at, cols]).astype(bf16)
            return moved, size

        zero = jnp.zeros((8, LANES), f32)
        moved, size = lax.fori_loop(0, dim // LANES, columns, (zero, zero), unroll=3)
        moved = jnp.sum(moved, axis=1, keepdims=True)
        size = jnp.sum(size, axis=1, keepdims=True)
        still = jnp.sum(jnp.where(moved <= size * (tolerance * tolerance), 0.0, 1.0))
        return done + 1, still

    lax.while_loop(
        lambda carry: jnp.logical_and(carry[0] < max_sweeps, carry[1] > 0.0),
        sweep,
        (jnp.int32(0), jnp.float32(1)),
    )

    def finish(n, _):
        cols = pl.ds(pl.multiple_of(n * LANES, LANES), LANES)
        acc = jnp.zeros((8, LANES), f32)
        for b in range(groups):
            at = slice(8 * b, 8 * b + 8)
            acc = acc + q_ref[at] * t[at, cols] * x_ref[at, cols]
        gain_sum[:, cols] = acc / gain_ref[0:1, cols]
        return 0

    lax.fori_loop(0, dim // LANES, finish, 0)
    left = LEFT
    right = small - left
    line = lax.broadcasted_iota(jnp.int32, (8, left), 0)
    total = jnp.sum(gain_sum[...], axis=0, keepdims=True)
    left_gain, right_gain = jnp.zeros((8, left), f32), jnp.zeros((8, right), f32)
    for k in range(LEFT_GAIN):
        left_gain = jnp.where(line == k, total[:, k * left : (k + 1) * left], left_gain)
    rest = dim - LEFT_GAIN * left
    for k in range(3):
        part = total[:, dim - rest + k * rest // 3 : dim - rest + (k + 1) * rest // 3]
        part = jnp.concatenate([part, jnp.zeros((1, right - rest // 3), f32)], axis=1)
        right_gain = jnp.where(line[:, :right] == k, part, right_gain)
    total = inject_sum[...]
    total = total + pltpu.roll(total, 4, 0)
    total = total + pltpu.roll(total, 2, 0)
    injects = []
    for half in range(Y_HI):
        lines = jnp.zeros((8, left), f32)
        for k in range(X):
            at = half * dim // 2 + k * eighth
            part = jnp.concatenate([total[:, at : at + eighth], jnp.zeros((8, left - eighth), f32)], axis=1)
            lines = jnp.where(line // 2 == k, part, lines)
        injects.append(lines)
    left_extra = jnp.concatenate(injects + [left_gain, jnp.zeros_like(left_gain)], axis=0).astype(bf16)
    right_extra = jnp.concatenate([right_gain, jnp.zeros_like(right_gain)], axis=0).astype(bf16)
    for own in range(4):

        @pl.when(shard == own)
        def _():
            for flip in range(4):
                at = (own ^ flip) * small
                outs[flip][0:rows] = v[:, at : at + left]
                outs[4 + flip][0:rows] = v[:, at + left : at + small]

    for flip in range(4):
        outs[flip][rows : rows + 32] = left_extra
        outs[4 + flip][rows : rows + 16] = right_extra


def solve(place, pieces, offsets, a, x, q, gain, final, tolerance):
    rows, dim = x.shape
    n = len(pieces)
    vm = pl.BlockSpec(memory_space=pltpu.VMEM)
    return pl.pallas_call(
        functools.partial(solve_kernel, offsets, 64, tolerance),
        out_shape=(jax.ShapeDtypeStruct((rows + 32, LEFT), bf16),) * 4
        + (jax.ShapeDtypeStruct((rows + 16, dim // 4 - LEFT), bf16),) * 4,
        in_specs=[pl.BlockSpec(memory_space=pltpu.SMEM)] + [pl.BlockSpec(memory_space=pl.ANY)] * n + [vm] * 5,
        out_specs=(vm,) * 8,
        scratch_shapes=[pltpu.VMEM((dim, dim), bf16)] * 2
        + [pltpu.VMEM((rows, dim), f32)] * 3
        + [pltpu.VMEM((rows, dim), bf16)]
        + [pltpu.VMEM((8, dim), f32)] * 3
        + [pltpu.SemaphoreType.DMA((n,))],
        compiler_params=pltpu.CompilerParams(vmem_limit_bytes=56 * 2**20),
        cost_estimate=pl.CostEstimate(flops=4 * 10**10, bytes_accessed=16 * 2**20, transcendentals=0),
    )(place, *pieces, a, x, q, gain, final)


def block_kernel(rows, dim, place_ref, a_ref, *refs):
    g_refs, out_ref, a, g, out, sems = refs[:X], refs[X], *refs[X + 1 :]
    part = dim // 64
    tall, cols = g_refs[0].shape[0] // 4, g_refs[0].shape[1]
    first = cols == LEFT
    place, shard = (place_ref[0] // Z) % X, place_ref[1]
    copies = []
    for step in range(X):
        copies.append(pltpu.make_async_copy(g_refs[step], g.at[step], sems.at[step]))
        for flip in range(4):
            source = lax.rem(place + (X - step), X) * 4 + lax.bitwise_xor(shard, flip)
            n = 4 * step + flip
            copies.append(pltpu.make_async_copy(a_ref.at[source], a.at[pl.ds(n * rows, rows)], sems.at[X + n]))
    for copy in copies:
        copy.start()
    for copy in copies:
        copy.wait()
    places = [(step, flip) for step in range(X) for flip in range(4)]
    right = jnp.concatenate([g[step, flip * tall : flip * tall + rows] for step, flip in places], axis=0)
    block = lax.dot_general(a[...], right, (((0,), (0,)), ((), ())), preferred_element_type=f32)
    gain = jnp.zeros((8, cols), f32)
    injects = []
    for step, flip in places:
        at = flip * tall + rows
        if not first:
            gain = gain + g[step, at : at + 16].astype(f32)[0:8]
            continue
        gain = gain + g[step, at + 16 : at + 32].astype(f32)[0:8]
        if flip == 0:
            lines = g[step, at : at + 16].astype(f32)
            own = [lines[8 * half : 8 * half + 2] for half in range(Y_HI)]
            for k in range(1, X):
                for half in range(Y_HI):
                    own[half] = jnp.where(place == k, lines[8 * half + 2 * k : 8 * half + 2 * k + 2], own[half])
            injects.append(own)
    for k in range(16):
        pieces = [block[k * part : (k + 1) * part]]
        if first:
            half, z = k // Z, k % Z
            inject = jnp.concatenate([own[half] for own in injects], axis=0)
            pieces.append(
                jnp.concatenate(
                    [inject[n : n + 1, z * part : (z + 1) * part] for n in range(8)]
                    + [jnp.zeros((1, cols - 8 * part), f32)],
                    axis=1,
                )
            )
        pieces.append(gain[0 : 48 - part - first])
        out[k] = jnp.concatenate(pieces, axis=0).astype(bf16)
    copy = pltpu.make_async_copy(out, out_ref, sems.at[X + 16])
    copy.start()
    copy.wait()


def block_sum(dim, place, a_all, g_parts):
    _, rows, wide = a_all.shape
    hold = pl.BlockSpec(memory_space=pl.ANY)
    return pl.pallas_call(
        functools.partial(block_kernel, rows, dim),
        out_shape=jax.ShapeDtypeStruct((16, 48, g_parts[0].shape[1]), bf16),
        in_specs=[pl.BlockSpec(memory_space=pltpu.SMEM)] + [hold] * (1 + X),
        out_specs=pl.BlockSpec(memory_space=pltpu.HBM),
        scratch_shapes=[
            pltpu.VMEM((16 * rows, wide), bf16),
            pltpu.VMEM((X,) + g_parts[0].shape, bf16),
            pltpu.VMEM((16, 48, g_parts[0].shape[1]), bf16),
            pltpu.SemaphoreType.DMA((X + 17,)),
        ],
        compiler_params=pltpu.CompilerParams(vmem_limit_bytes=48 * 2**20),
        cost_estimate=pl.CostEstimate(flops=4 * 10**9, bytes_accessed=6 * 2**20, transcendentals=0),
    )(place, a_all, *g_parts)


def flat(y, x, z, core):
    return (((y // Y_LO) * X + x) * Z + z) * 4 + (y % Y_LO) * CORE + core


PLACES = [
    (y, x, z, core)
    for y in range(Y_HI * Y_LO)
    for x in range(X)
    for z in range(Z)
    for core in range(CORE)
]


def move(value, target):
    return lax.ppermute(value, AXES, [(flat(*place), flat(*target(*place))) for place in PLACES])


def y_move(value, steps):
    return move(value, lambda y, x, z, core: ((y + steps) % (Y_HI * Y_LO), x, z, core))


def x_move(value, steps):
    return move(value, lambda y, x, z, core: (y, (x + steps) % X, z, core))


def dp_move(value, flip):
    return move(value, lambda y, x, z, core: (y ^ (flip // CORE), x, z, core ^ (flip % CORE)))


XD_GROUPS = [
    [flat(yh * Y_LO + d // CORE, x, z, d % CORE) for x in range(X) for d in range(4)]
    for yh in range(Y_HI)
    for z in range(Z)
]
YZ_GROUPS = [
    [flat(yh * Y_LO + d // CORE, x, z, d % CORE) for yh in range(Y_HI) for z in range(Z)]
    for x in range(X)
    for d in range(4)
]


def gather_weight(weight, meanwhile):
    half = weight.shape[0] // 2
    pieces, offsets = [weight, dp_move(weight, 1)], [(0, 0, 2 * half), (1, 0, 2 * half)]
    source = weight
    cuts = (0, 112, 240, 336)
    for low, high in zip(cuts[:-1], cuts[1:]):
        if high == half:
            other = meanwhile()
            source, other = lax.optimization_barrier((source, other))
        up, down = y_move(source[low:high], 1), y_move(source[half + low : half + high], -1)
        source, up, down = lax.optimization_barrier((source, up, down))
        for piece, start in ((up, low), (down, half + low)):
            pieces += [piece, dp_move(piece, 1)]
            offsets += [(2, start, high - low), (3, start, high - low)]
    return pieces, tuple(offsets), other


def per_device(states, inject, final_cotangent, weight, norm_gain):
    micro_count, row_count, dim = inject.shape
    sections = lax.axis_size("section")
    section, shard = lax.axis_index("section"), lax.axis_index("dp")
    own = micro_count * row_count // sections
    place = jnp.stack([section, shard]).astype(jnp.int32)
    gain = norm_gain.reshape(1, dim)

    def meanwhile():
        mine = lax.all_to_all(states[0].reshape(sections, own, dim), "section", 0, 0)
        return prepare(place, mine, inject, gain)

    pieces, offsets, (x, a, q, a_cut) = gather_weight(weight, meanwhile)

    a_all = lax.all_to_all(a_cut, AXES, 0, 0, axis_index_groups=XD_GROUPS)

    g_parts = solve(place, pieces, offsets, a, x, q, gain, final_cotangent, TOLERANCE)

    a_all, g_parts = lax.optimization_barrier((a_all, g_parts))
    sums = []
    for n in range(2):
        near = g_parts[4 * n : 4 * n + 4]
        near = jnp.concatenate([near[0]] + [dp_move(near[flip], flip) for flip in (1, 2, 3)])
        out = block_sum(dim, place, a_all, [near] + [x_move(near, step) for step in range(1, X)])
        sums.append(lax.all_to_all(out, AXES, 0, 0, axis_index_groups=YZ_GROUPS))
    part = dim // 64
    total = [jnp.sum(value.astype(f32), axis=0) for value in sums]
    d_weight = jnp.concatenate([value[:part] for value in total], axis=1)
    rest = dim - LEFT_GAIN * LEFT
    d_gain = jnp.concatenate(
        [total[0][part + 1 : part + 1 + LEFT_GAIN].reshape(-1), total[1][part : part + 3, : rest // 3].reshape(-1)]
    )
    d_inject = sums[0][:, part, : X * own * part].reshape(Y_HI, Z, X, own, part)
    d_inject = jnp.roll(d_inject[:, :, ::-1], (section // Z) % X + 1, axis=2).transpose(0, 2, 1, 3, 4)
    d_inject = d_inject.reshape(micro_count, row_count, part).astype(f32)
    return d_inject, d_weight, d_gain


def solution(mesh):
    in_specs = (
        P("section", None, "dp", None),
        P(None, "dp", None),
        P(None, "dp", None),
        P("dp", None),
        P(),
    )
    out_specs = (P(None, "dp", "section"), P("section", "dp"), P())
    return jax.shard_map(
        per_device, mesh=mesh, in_specs=in_specs, out_specs=out_specs, check_vma=False
    )
```

```python
import functools
import math

import jax
import jax.numpy as jnp
from jax import lax
from jax.experimental import pallas as pl
from jax.experimental.pallas import tpu as pltpu
from jax.sharding import PartitionSpec as P

EPSILON = 1e-06
TOLERANCE = 2.0**-10
LANES = 128
WIDE = 512
AXES = ("section", "dp")
Y_HI, X, Z, Y_LO, CORE = 2, 4, 8, 2, 2
f32, bf16 = jnp.float32, jnp.bfloat16


def own_tokens(ref, section, copies):
    block = ref[section // 4].astype(f32)
    pair = block[0:2]
    for k in range(1, 4):
        pair = jnp.where(section % 4 == k, block[2 * k : 2 * k + 2], pair)
    return jnp.concatenate([pair] * copies, axis=0)


def prepare_kernel(place_ref, states_ref, inject_ref, gain_ref, x_ref, a_ref, q_ref, *cut_refs):
    rows, dim = x_ref.shape
    section = place_ref[0]
    inject = own_tokens(inject_ref, section, 4)
    gain = gain_ref[...]
    groups = rows // 8

    def one(b, _):
        x = jnp.concatenate([states_ref[seg * groups + b].astype(f32) for seg in range(4)], axis=0) + inject
        q = lax.rsqrt(jnp.sum(x * x, axis=1, keepdims=True) * (1.0 / dim) + EPSILON)
        at = pl.ds(pl.multiple_of(b * 8, 8), 8)
        x_ref[at, :] = x
        q_ref[at, :] = jnp.broadcast_to(q, (8, LANES))
        return 0

    lax.fori_loop(0, groups, one, 0)
    a_ref[...] = (x_ref[...] * q_ref[:, 0:1] * gain).astype(bf16)
    eighth = dim // 8
    place = (section // Z) % X
    for cut_ref in cut_refs:
        cut_ref[:, 2 * eighth :] = jnp.zeros((rows, cut_ref.shape[1] - 2 * eighth), bf16)
    for own in range(X):

        @pl.when(place == own)
        def _():
            for step in range(X):
                k = (own + step) % X
                cut_refs[step][:, 0:eighth] = a_ref[:, k * eighth : (k + 1) * eighth]
                cut_refs[step][:, eighth : 2 * eighth] = a_ref[:, dim // 2 + k * eighth : dim // 2 + (k + 1) * eighth]


def prepare(place, states, inject, gain):
    rows, dim = states.shape[0] * states.shape[1], states.shape[2]
    vm = pl.BlockSpec(memory_space=pltpu.VMEM)
    return pl.pallas_call(
        prepare_kernel,
        out_shape=(
            jax.ShapeDtypeStruct((rows, dim), f32),
            jax.ShapeDtypeStruct((rows, dim), bf16),
            jax.ShapeDtypeStruct((rows, LANES), f32),
        )
        + (jax.ShapeDtypeStruct((rows, pl.cdiv(dim // 4, LANES) * LANES), bf16),) * X,
        in_specs=[pl.BlockSpec(memory_space=pltpu.SMEM)] + [vm] * 3,
        out_specs=(vm,) * (3 + X),
        compiler_params=pltpu.CompilerParams(vmem_limit_bytes=32 * 2**20),
        cost_estimate=pl.CostEstimate(flops=20 * 10**9, bytes_accessed=4 * 2**20, transcendentals=0),
    )(place, states, inject, gain)


def solve_kernel(offsets, max_sweeps, tolerance, place_ref, *refs):
    count = len(offsets)
    pieces = refs[:count]
    a_ref, x_ref, q_ref, gain_ref, final_ref = refs[count : count + 5]
    outs = refs[count + 5 : count + 9]
    w, wt, slope, t, p, v, inject_sum, gain_sum, final, sems = refs[count + 9 :]
    rows, dim = x_ref.shape
    section, shard = place_ref[0], place_ref[1]
    small, eighth, groups = dim // 4, dim // 8, rows // 8

    blocks = [(low, min(WIDE, dim - low)) for low in range(0, dim, WIDE)]
    copies = {}
    for m, (low, width) in enumerate(blocks):
        for n, ((flip, start, length), piece) in enumerate(zip(offsets, pieces)):
            at = pl.multiple_of(lax.bitwise_xor(shard, flip) * small + start, 16)
            copies[m, n] = pltpu.make_async_copy(
                piece.at[:, pl.ds(low, width)], w.at[pl.ds(at, length), pl.ds(low, width)], sems.at[m, n]
            )
            copies[m, n].start()
    final[...] = own_tokens(final_ref, section, 4)
    p[...] = jnp.zeros_like(p)
    for m, (low, width) in enumerate(blocks):
        for n in range(count):
            copies[m, n].wait()
        cols = slice(low, low + width)
        h = jnp.dot(a_ref[...], w[:, cols], preferred_element_type=f32)
        s = jax.nn.sigmoid(h)
        sl = s * (1.0 + h * (1.0 - s)) * (1.0 / math.sqrt(max_sweeps))
        slope[:, cols] = sl
        v[:, cols] = (sl * jnp.concatenate([final[:, cols]] * groups, axis=0)).astype(bf16)
        wt[cols, :] = w[:, cols].T
    sub = lax.broadcasted_iota(jnp.int32, (8, LANES), 0)

    def sweep(carry):
        done, _ = carry
        acc = jnp.zeros((rows, LANES), f32)
        for j, width in blocks:
            cols = slice(j, j + width)
            u = jnp.dot(v[...], wt[:, cols], preferred_element_type=f32)
            scaled = u * gain_ref[0:1, cols]
            t[:, cols] = scaled
            scaled = scaled * x_ref[:, cols]
            for k in range(0, width, LANES):
                acc = acc + scaled[:, k : k + LANES]
        q = q_ref[...]
        kappa = q * q * q * (jnp.sum(acc, axis=1, keepdims=True) * (1.0 / dim))

        def columns(n, sums):
            moved, size = sums
            cols = pl.ds(pl.multiple_of(n * LANES, LANES), LANES)
            run, tails = None, [None] * groups
            for b in range(groups - 1, -1, -1):
                at = slice(8 * b, 8 * b + 8)
                new = q[at] * t[at, cols] - kappa[at] * x_ref[at, cols]
                step = new - p[at, cols]
                p[at, cols] = new
                moved = moved + step * step
                run = new if run is None else run + new
                tails[b] = run
            inject_sum[:, cols] = run
            base = final[:, cols]
            for k in (2, 4, 6):
                base = base + jnp.where(sub < 8 - k, pltpu.roll(run, 8 - k, 0), 0.0)
            for b in range(groups):
                at = slice(8 * b, 8 * b + 8)
                c = base if b == groups - 1 else base + tails[b + 1]
                size = size + c * c
                v[at, cols] = (c * slope[at, cols]).astype(bf16)
            return moved, size

        zero = jnp.zeros((8, LANES), f32)
        moved, size = lax.fori_loop(0, dim // LANES, columns, (zero, zero), unroll=3)
        moved = jnp.sum(moved, axis=1, keepdims=True)
        size = jnp.sum(size, axis=1, keepdims=True)
        still = jnp.sum(jnp.where(moved <= size * (tolerance * tolerance), 0.0, 1.0))
        return done + 1, still

    lax.while_loop(
        lambda carry: jnp.logical_and(carry[0] < max_sweeps, carry[1] > 0.0),
        sweep,
        (jnp.int32(0), jnp.float32(1)),
    )

    def finish(n, _):
        cols = pl.ds(pl.multiple_of(n * LANES, LANES), LANES)
        acc = jnp.zeros((8, LANES), f32)
        for b in range(groups):
            at = slice(8 * b, 8 * b + 8)
            acc = acc + q_ref[at] * t[at, cols] * x_ref[at, cols]
        gain_sum[:, cols] = acc / gain_ref[0:1, cols]
        return 0

    lax.fori_loop(0, dim // LANES, finish, 0)
    wide_sub = lax.broadcasted_iota(jnp.int32, (8, small), 0)
    gain_rows = jnp.zeros((8, small), f32)
    total = jnp.sum(gain_sum[...], axis=0, keepdims=True)
    for k in range(4):
        gain_rows = jnp.where(wide_sub == k, total[:, k * small : (k + 1) * small], gain_rows)
    inject_rows = jnp.zeros((8, small), f32)
    total = inject_sum[...]
    total = total + pltpu.roll(total, 4, 0)
    total = total + pltpu.roll(total, 2, 0)
    for k in range(X):
        part = jnp.concatenate(
            [total[:, k * eighth : (k + 1) * eighth], total[:, dim // 2 + k * eighth : dim // 2 + (k + 1) * eighth]],
            axis=1,
        )
        inject_rows = jnp.where(wide_sub // 2 == k, part, inject_rows)
    extra = jnp.concatenate([inject_rows, gain_rows], axis=0).astype(bf16)
    for own in range(4):

        @pl.when(shard == own)
        def _():
            for flip in range(4):
                block = own ^ flip
                outs[flip][0:rows] = v[:, block * small : (block + 1) * small]

    for flip in range(4):
        outs[flip][rows : rows + 16] = extra


def solve(place, pieces, offsets, a, x, q, gain, final, tolerance):
    rows, dim = x.shape
    n = len(pieces)
    vm = pl.BlockSpec(memory_space=pltpu.VMEM)
    return pl.pallas_call(
        functools.partial(solve_kernel, offsets, 64, tolerance),
        out_shape=(jax.ShapeDtypeStruct((rows + 16, dim // 4), bf16),) * 4,
        in_specs=[pl.BlockSpec(memory_space=pltpu.SMEM)] + [pl.BlockSpec(memory_space=pl.ANY)] * n + [vm] * 5,
        out_specs=(vm,) * 4,
        scratch_shapes=[pltpu.VMEM((dim, dim), bf16)] * 2
        + [pltpu.VMEM((rows, dim), f32)] * 3
        + [pltpu.VMEM((rows, dim), bf16)]
        + [pltpu.VMEM((8, dim), f32)] * 3
        + [pltpu.SemaphoreType.DMA((pl.cdiv(dim, WIDE), n))],
        compiler_params=pltpu.CompilerParams(vmem_limit_bytes=56 * 2**20),
        cost_estimate=pl.CostEstimate(flops=4 * 10**10, bytes_accessed=16 * 2**20, transcendentals=0),
    )(place, *pieces, a, x, q, gain, final)


def block_kernel(rows, dim, place_ref, *refs):
    a_refs, own_refs, core_refs, chip_refs = refs[:4], refs[4:8], refs[8:12], refs[12:16]
    same_ref, other_ref, a, g, sems = refs[16:]
    small, part = dim // 4, dim // 64
    tall = rows + 16
    copies = [pltpu.make_async_copy(a_refs[flip], a.at[pl.ds(flip * X * rows, X * rows)], sems.at[flip]) for flip in range(4)]
    for step in range(X):
        for n, ref in ((0, own_refs[step]), (1, core_refs[step]), (2, chip_refs[step])):
            at = pl.ds((4 * step + n) * tall, ref.shape[0])
            copies.append(pltpu.make_async_copy(ref, g.at[at], sems.at[4 + 3 * step + n]))
    for copy in copies:
        copy.start()
    for copy in copies:
        copy.wait()

    places = [(flip, step) for flip in range(4) for step in range(X)]
    starts = [(4 * step + flip) * tall for flip, step in places]
    right = jnp.concatenate([g[start : start + rows] for start in starts], axis=0)
    block = lax.dot_general(a[...], right, (((0,), (0,)), ((), ())), preferred_element_type=f32)
    gain = jnp.zeros((8, small), f32)
    injects = []
    place = (place_ref[0] // Z) % X
    for (flip, step), start in zip(places, starts):
        extra = g[start + rows : start + tall].astype(f32)
        gain = gain + extra[8:16]
        if flip == 0:
            own = extra[0:2]
            for k in range(1, X):
                own = jnp.where(place == k, extra[2 * k : 2 * k + 2], own)
            injects.append(own)
    inject = jnp.concatenate(injects, axis=0)
    none = jnp.zeros((1, small), f32)
    for half in range(Y_HI):
        for z in range(Z):
            k = half * Z + z
            line = jnp.concatenate(
                [inject[n : n + 1, k * part : (k + 1) * part] for n in range(8)]
                + [jnp.zeros((1, small - 8 * part), f32)],
                axis=1,
            )
            rest = block[k * part : (k + 1) * part]

            @pl.when(place_ref[0] // (X * Z) == half)
            def _():
                same_ref[z] = jnp.concatenate([rest, line, none, gain[0:4]], axis=0).astype(bf16)

            @pl.when(place_ref[0] // (X * Z) != half)
            def _():
                other_ref[z] = jnp.concatenate([rest, none, line, gain[0:4]], axis=0).astype(bf16)


def block_sum(place, a_parts, own_parts, core_parts, chip_parts):
    rows, small = a_parts[0].shape[0] // X, own_parts[0].shape[1]
    hold = pl.BlockSpec(memory_space=pl.ANY)
    return pl.pallas_call(
        functools.partial(block_kernel, rows, 4 * small),
        out_shape=(jax.ShapeDtypeStruct((Z, 48, small), bf16),) * 2,
        in_specs=[pl.BlockSpec(memory_space=pltpu.SMEM)] + [hold] * 16,
        out_specs=(pl.BlockSpec(memory_space=pltpu.VMEM),) * 2,
        scratch_shapes=[
            pltpu.VMEM((16 * rows, a_parts[0].shape[1]), bf16),
            pltpu.VMEM((16 * (rows + 16), small), bf16),
            pltpu.SemaphoreType.DMA((16,)),
        ],
        compiler_params=pltpu.CompilerParams(vmem_limit_bytes=48 * 2**20),
    )(place, *a_parts, *own_parts, *core_parts, *chip_parts)


def flat(y, x, z, core):
    return (((y // Y_LO) * X + x) * Z + z) * 4 + (y % Y_LO) * CORE + core


PLACES = [
    (y, x, z, core)
    for y in range(Y_HI * Y_LO)
    for x in range(X)
    for z in range(Z)
    for core in range(CORE)
]


def move(value, target):
    return lax.ppermute(value, AXES, [(flat(*place), flat(*target(*place))) for place in PLACES])


def y_move(value, steps):
    return move(value, lambda y, x, z, core: ((y + steps) % (Y_HI * Y_LO), x, z, core))


def x_move(value, steps):
    return move(value, lambda y, x, z, core: (y, (x + steps) % X, z, core))


def dp_move(value, flip):
    return move(value, lambda y, x, z, core: (y ^ (flip // CORE), x, z, core ^ (flip % CORE)))


Z_GROUPS = [
    [flat(yh * Y_LO + d // CORE, x, z, d % CORE) for z in range(Z)]
    for yh in range(Y_HI)
    for x in range(X)
    for d in range(4)
]


def gather_weight(weight):
    half = weight.shape[0] // 2
    pieces, offsets = [weight, dp_move(weight, 1)], [(0, 0, 2 * half), (1, 0, 2 * half)]
    source = weight
    cuts = (0, 128, 240, 336)
    for low, high in zip(cuts[:-1], cuts[1:]):
        up, down = y_move(source[low:high], 1), y_move(source[half + low : half + high], -1)
        source, up, down = lax.optimization_barrier((source, up, down))
        for piece, start in ((up, low), (down, half + low)):
            pieces += [piece, dp_move(piece, 1)]
            offsets += [(2, start, high - low), (3, start, high - low)]
    return pieces, tuple(offsets)


def per_device(states, inject, final_cotangent, weight, norm_gain):
    micro_count, row_count, dim = inject.shape
    sections = lax.axis_size("section")
    section, shard = lax.axis_index("section"), lax.axis_index("dp")
    own = micro_count * row_count // sections
    place = jnp.stack([section, shard]).astype(jnp.int32)
    gain = norm_gain.reshape(1, dim)
    pieces, offsets = gather_weight(weight)

    mine = lax.all_to_all(states[0].reshape(sections, own, dim), "section", 0, 0)
    x, a, q, *a_cut = prepare(place, mine, inject, gain)

    a_ring = jnp.concatenate([a_cut[0]] + [x_move(a_cut[step], step) for step in range(1, X)])
    a_parts = [a_ring] + [dp_move(a_ring, flip) for flip in (1, 2, 3)]

    g_parts = solve(place, pieces, offsets, a, x, q, gain, final_cotangent, TOLERANCE)

    a_parts, g_parts = lax.optimization_barrier((a_parts, g_parts))
    core_part, chip_part, chip_more = (dp_move(g_parts[flip], flip) for flip in (1, 2, 3))
    own_parts = [g_parts[0]] + [x_move(g_parts[0], step) for step in range(1, X)]
    core_parts = [core_part] + [x_move(core_part, step) for step in range(1, X)]
    chip_part = jnp.concatenate([chip_part, chip_more])
    chip_part, _, _ = lax.optimization_barrier((chip_part, own_parts, core_part))
    chip_parts = [chip_part] + [x_move(chip_part, step) for step in range(1, X)]
    same, other = block_sum(place, a_parts, own_parts, core_parts, chip_parts)

    got = (same.astype(f32) + y_move(other, Y_LO).astype(f32)).astype(bf16)
    got = lax.all_to_all(got, AXES, 0, 0, axis_index_groups=Z_GROUPS)
    part = dim // 64
    total = jnp.sum(got.astype(f32), axis=0)
    d_weight = total[:part]
    d_gain = total[part + 2 : part + 6].reshape(dim)
    d_inject = got[:, part : part + 2, : X * own * part].reshape(Z, Y_HI, X, own, part)
    d_inject = jnp.roll(d_inject, section // (X * Z), axis=1)
    d_inject = jnp.roll(d_inject[:, :, ::-1], (section // Z) % X + 1, axis=2).transpose(1, 2, 0, 3, 4)
    d_inject = d_inject.reshape(micro_count, row_count, part).astype(f32)
    return d_inject, d_weight, d_gain


def solution(mesh):
    in_specs = (
        P("section", None, "dp", None),
        P(None, "dp", None),
        P(None, "dp", None),
        P("dp", None),
        P(),
    )
    out_specs = (P(None, "dp", "section"), P("section", "dp"), P())
    return jax.shard_map(
        per_device, mesh=mesh, in_specs=in_specs, out_specs=out_specs, check_vma=False
    )
```

```python
import functools
import math

import jax
import jax.numpy as jnp
from jax import lax
from jax.experimental import pallas as pl
from jax.experimental.pallas import tpu as pltpu
from jax.sharding import PartitionSpec as P

EPSILON = 1e-06
TOLERANCE = 2.0**-10
LANES = 128
WIDE = 512
AXES = ("section", "dp")
Y_HI, X, Z, Y_LO, CORE = 2, 4, 8, 2, 2
f32, bf16 = jnp.float32, jnp.bfloat16


def own_tokens(ref, section, copies):
    block = ref[section // 4].astype(f32)
    pair = block[0:2]
    for k in range(1, 4):
        pair = jnp.where(section % 4 == k, block[2 * k : 2 * k + 2], pair)
    return jnp.concatenate([pair] * copies, axis=0)


def prepare_kernel(place_ref, states_ref, inject_ref, gain_ref, x_ref, a_ref, q_ref, *cut_refs):
    rows, dim = x_ref.shape
    section = place_ref[0]
    inject = own_tokens(inject_ref, section, 4)
    gain = gain_ref[...]
    groups = rows // 8

    def one(b, _):
        x = jnp.concatenate([states_ref[seg * groups + b].astype(f32) for seg in range(4)], axis=0) + inject
        q = lax.rsqrt(jnp.sum(x * x, axis=1, keepdims=True) * (1.0 / dim) + EPSILON)
        at = pl.ds(pl.multiple_of(b * 8, 8), 8)
        x_ref[at, :] = x
        q_ref[at, :] = jnp.broadcast_to(q, (8, LANES))
        return 0

    lax.fori_loop(0, groups, one, 0)
    a_ref[...] = (x_ref[...] * q_ref[:, 0:1] * gain).astype(bf16)
    eighth = dim // 8
    place = (section // Z) % X
    for cut_ref in cut_refs:
        cut_ref[:, 2 * eighth :] = jnp.zeros((rows, cut_ref.shape[1] - 2 * eighth), bf16)
    for own in range(X):

        @pl.when(place == own)
        def _():
            for step in range(X):
                k = (own + step) % X
                cut_refs[step][:, 0:eighth] = a_ref[:, k * eighth : (k + 1) * eighth]
                cut_refs[step][:, eighth : 2 * eighth] = a_ref[:, dim // 2 + k * eighth : dim // 2 + (k + 1) * eighth]


def prepare(place, states, inject, gain):
    rows, dim = states.shape[0] * states.shape[1], states.shape[2]
    vm = pl.BlockSpec(memory_space=pltpu.VMEM)
    return pl.pallas_call(
        prepare_kernel,
        out_shape=(
            jax.ShapeDtypeStruct((rows, dim), f32),
            jax.ShapeDtypeStruct((rows, dim), bf16),
            jax.ShapeDtypeStruct((rows, LANES), f32),
        )
        + (jax.ShapeDtypeStruct((rows, pl.cdiv(dim // 4, LANES) * LANES), bf16),) * X,
        in_specs=[pl.BlockSpec(memory_space=pltpu.SMEM)] + [vm] * 3,
        out_specs=(vm,) * (3 + X),
        compiler_params=pltpu.CompilerParams(vmem_limit_bytes=32 * 2**20),
        cost_estimate=pl.CostEstimate(flops=20 * 10**9, bytes_accessed=4 * 2**20, transcendentals=0),
    )(place, states, inject, gain)


def solve_kernel(offsets, max_sweeps, tolerance, place_ref, *refs):
    count = len(offsets)
    pieces = refs[:count]
    a_ref, x_ref, q_ref, gain_ref, final_ref = refs[count : count + 5]
    outs = refs[count + 5 : count + 9]
    w, wt, slope, t, p, v, inject_sum, gain_sum, final, sems = refs[count + 9 :]
    rows, dim = x_ref.shape
    section, shard = place_ref[0], place_ref[1]
    small, eighth, groups = dim // 4, dim // 8, rows // 8

    blocks = [(low, min(WIDE, dim - low)) for low in range(0, dim, WIDE)]
    copies = {}
    for m, (low, width) in enumerate(blocks):
        for n, ((flip, start, length), piece) in enumerate(zip(offsets, pieces)):
            at = pl.multiple_of(lax.bitwise_xor(shard, flip) * small + start, 16)
            copies[m, n] = pltpu.make_async_copy(
                piece.at[:, pl.ds(low, width)], w.at[pl.ds(at, length), pl.ds(low, width)], sems.at[m, n]
            )
            copies[m, n].start()
    final[...] = own_tokens(final_ref, section, 4)
    p[...] = jnp.zeros_like(p)
    for m, (low, width) in enumerate(blocks):
        for n in range(count):
            copies[m, n].wait()
        cols = slice(low, low + width)
        h = jnp.dot(a_ref[...], w[:, cols], preferred_element_type=f32)
        s = jax.nn.sigmoid(h)
        sl = s * (1.0 + h * (1.0 - s)) * (1.0 / math.sqrt(max_sweeps))
        slope[:, cols] = sl
        v[:, cols] = (sl * jnp.concatenate([final[:, cols]] * groups, axis=0)).astype(bf16)
        wt[cols, :] = w[:, cols].T
    sub = lax.broadcasted_iota(jnp.int32, (8, LANES), 0)

    def sweep(carry):
        done, _ = carry
        acc = jnp.zeros((rows, LANES), f32)
        for j, width in blocks:
            cols = slice(j, j + width)
            u = jnp.dot(v[...], wt[:, cols], preferred_element_type=f32)
            scaled = u * gain_ref[0:1, cols]
            t[:, cols] = scaled
            scaled = scaled * x_ref[:, cols]
            for k in range(0, width, LANES):
                acc = acc + scaled[:, k : k + LANES]
        q = q_ref[...]
        kappa = q * q * q * (jnp.sum(acc, axis=1, keepdims=True) * (1.0 / dim))

        def columns(n, sums):
            moved, size = sums
            cols = pl.ds(pl.multiple_of(n * LANES, LANES), LANES)
            run, tails = None, [None] * groups
            for b in range(groups - 1, -1, -1):
                at = slice(8 * b, 8 * b + 8)
                new = q[at] * t[at, cols] - kappa[at] * x_ref[at, cols]
                step = new - p[at, cols]
                p[at, cols] = new
                moved = moved + step * step
                run = new if run is None else run + new
                tails[b] = run
            inject_sum[:, cols] = run
            base = final[:, cols]
            for k in (2, 4, 6):
                base = base + jnp.where(sub < 8 - k, pltpu.roll(run, 8 - k, 0), 0.0)
            for b in range(groups):
                at = slice(8 * b, 8 * b + 8)
                c = base if b == groups - 1 else base + tails[b + 1]
                size = size + c * c
                v[at, cols] = (c * slope[at, cols]).astype(bf16)
            return moved, size

        zero = jnp.zeros((8, LANES), f32)
        moved, size = lax.fori_loop(0, dim // LANES, columns, (zero, zero), unroll=3)
        moved = jnp.sum(moved, axis=1, keepdims=True)
        size = jnp.sum(size, axis=1, keepdims=True)
        still = jnp.sum(jnp.where(moved <= size * (tolerance * tolerance), 0.0, 1.0))
        return done + 1, still

    lax.while_loop(
        lambda carry: jnp.logical_and(carry[0] < max_sweeps, carry[1] > 0.0),
        sweep,
        (jnp.int32(0), jnp.float32(1)),
    )

    def finish(n, _):
        cols = pl.ds(pl.multiple_of(n * LANES, LANES), LANES)
        acc = jnp.zeros((8, LANES), f32)
        for b in range(groups):
            at = slice(8 * b, 8 * b + 8)
            acc = acc + q_ref[at] * t[at, cols] * x_ref[at, cols]
        gain_sum[:, cols] = acc / gain_ref[0:1, cols]
        return 0

    lax.fori_loop(0, dim // LANES, finish, 0)
    wide_sub = lax.broadcasted_iota(jnp.int32, (8, small), 0)
    gain_rows = jnp.zeros((8, small), f32)
    total = jnp.sum(gain_sum[...], axis=0, keepdims=True)
    for k in range(4):
        gain_rows = jnp.where(wide_sub == k, total[:, k * small : (k + 1) * small], gain_rows)
    inject_rows = jnp.zeros((8, small), f32)
    total = inject_sum[...]
    total = total + pltpu.roll(total, 4, 0)
    total = total + pltpu.roll(total, 2, 0)
    for k in range(X):
        part = jnp.concatenate(
            [total[:, k * eighth : (k + 1) * eighth], total[:, dim // 2 + k * eighth : dim // 2 + (k + 1) * eighth]],
            axis=1,
        )
        inject_rows = jnp.where(wide_sub // 2 == k, part, inject_rows)
    extra = jnp.concatenate([inject_rows, gain_rows], axis=0).astype(bf16)
    for own in range(4):

        @pl.when(shard == own)
        def _():
            for flip in range(4):
                block = own ^ flip
                outs[flip][0:rows] = v[:, block * small : (block + 1) * small]

    for flip in range(4):
        outs[flip][rows : rows + 16] = extra


def solve(place, pieces, offsets, a, x, q, gain, final, tolerance):
    rows, dim = x.shape
    n = len(pieces)
    vm = pl.BlockSpec(memory_space=pltpu.VMEM)
    return pl.pallas_call(
        functools.partial(solve_kernel, offsets, 64, tolerance),
        out_shape=(jax.ShapeDtypeStruct((rows + 16, dim // 4), bf16),) * 4,
        in_specs=[pl.BlockSpec(memory_space=pltpu.SMEM)] + [pl.BlockSpec(memory_space=pl.ANY)] * n + [vm] * 5,
        out_specs=(vm,) * 4,
        scratch_shapes=[pltpu.VMEM((dim, dim), bf16)] * 2
        + [pltpu.VMEM((rows, dim), f32)] * 3
        + [pltpu.VMEM((rows, dim), bf16)]
        + [pltpu.VMEM((8, dim), f32)] * 3
        + [pltpu.SemaphoreType.DMA((pl.cdiv(dim, WIDE), n))],
        compiler_params=pltpu.CompilerParams(vmem_limit_bytes=56 * 2**20),
        cost_estimate=pl.CostEstimate(flops=4 * 10**10, bytes_accessed=16 * 2**20, transcendentals=0),
    )(place, *pieces, a, x, q, gain, final)


def block_kernel(rows, dim, place_ref, *refs):
    a_refs, own_refs, far_refs = refs[:4], refs[4:8], refs[8:12]
    out_ref, a, g, sems = refs[12:]
    small, part = dim // 4, dim // 64
    tall = rows + 16
    copies = [pltpu.make_async_copy(a_refs[flip], a.at[flip], sems.at[flip]) for flip in range(4)]
    for step in range(X):
        copies.append(pltpu.make_async_copy(own_refs[step], g.at[pl.ds(step * tall, tall)], sems.at[4 + step]))
        copies.append(pltpu.make_async_copy(far_refs[step], g.at[pl.ds((4 + 3 * step) * tall, 3 * tall)], sems.at[8 + step]))
    for copy in copies:
        copy.start()
    for copy in copies:
        copy.wait()

    def slot(flip, step):
        return tall * (step if flip == 0 else 3 + 3 * step + flip)

    places = [(flip, step) for flip in range(4) for step in range(X)]
    left = jnp.concatenate([a[flip, step * rows : (step + 1) * rows] for flip, step in places], axis=0)
    right = jnp.concatenate([g[slot(flip, step) : slot(flip, step) + rows] for flip, step in places], axis=0)
    block = lax.dot_general(left, right, (((0,), (0,)), ((), ())), preferred_element_type=f32)
    gain = jnp.zeros((8, small), f32)
    injects = []
    for flip, step in places:
        extra = g[slot(flip, step) + rows : slot(flip, step) + tall].astype(f32)
        gain = gain + extra[8:16]
        if flip == 0:
            own = extra[0:2]
            for k in range(1, X):
                own = jnp.where((place_ref[0] // Z) % X == k, extra[2 * k : 2 * k + 2], own)
            injects.append(own)
    inject = jnp.concatenate(injects, axis=0)
    for k in range(16):
        line = jnp.concatenate(
            [inject[n : n + 1, k * part : (k + 1) * part] for n in range(8)] + [jnp.zeros((1, small - 8 * part), f32)],
            axis=1,
        )
        out_ref[k] = jnp.concatenate([block[k * part : (k + 1) * part], line, gain[0:5]], axis=0).astype(bf16)


def block_sum(place, a_parts, own_parts, far_parts):
    rows, small = a_parts[0].shape[0] // X, own_parts[0].shape[1]
    hold = pl.BlockSpec(memory_space=pl.ANY)
    return pl.pallas_call(
        functools.partial(block_kernel, rows, 4 * small),
        out_shape=jax.ShapeDtypeStruct((16, 48, small), bf16),
        in_specs=[pl.BlockSpec(memory_space=pltpu.SMEM)] + [hold] * 12,
        out_specs=pl.BlockSpec(memory_space=pltpu.VMEM),
        scratch_shapes=[
            pltpu.VMEM((4,) + a_parts[0].shape, bf16),
            pltpu.VMEM((16 * (rows + 16), small), bf16),
            pltpu.SemaphoreType.DMA((12,)),
        ],
        compiler_params=pltpu.CompilerParams(vmem_limit_bytes=48 * 2**20),
    )(place, *a_parts, *own_parts, *far_parts)


def flat(y, x, z, core):
    return (((y // Y_LO) * X + x) * Z + z) * 4 + (y % Y_LO) * CORE + core


PLACES = [
    (y, x, z, core)
    for y in range(Y_HI * Y_LO)
    for x in range(X)
    for z in range(Z)
    for core in range(CORE)
]


def move(value, target):
    return lax.ppermute(value, AXES, [(flat(*place), flat(*target(*place))) for place in PLACES])


def y_move(value, steps):
    return move(value, lambda y, x, z, core: ((y + steps) % (Y_HI * Y_LO), x, z, core))


def x_move(value, steps):
    return move(value, lambda y, x, z, core: (y, (x + steps) % X, z, core))


def dp_move(value, flip):
    return move(value, lambda y, x, z, core: (y ^ (flip // CORE), x, z, core ^ (flip % CORE)))


YZ_GROUPS = [
    [flat(yh * Y_LO + d // CORE, x, z, d % CORE) for yh in range(Y_HI) for z in range(Z)]
    for x in range(X)
    for d in range(4)
]


def fetch_weight(weight):
    half = weight.shape[0] // 2
    cuts = (0, 128, 336)
    source, landed = weight, []
    for low, high in zip(cuts[:-1], cuts[1:]):
        up, down = y_move(source[low:high], 1), y_move(source[half + low : half + high], -1)
        source, up, down = lax.optimization_barrier((source, up, down))
        landed += [(low, up), (half + low, down)]
    return landed


def share_weight(weight, landed):
    pieces, offsets = [weight, dp_move(weight, 1)], [(0, 0, weight.shape[0]), (1, 0, weight.shape[0])]
    for start, piece in landed:
        pieces += [piece, dp_move(piece, 1)]
        offsets += [(2, start, piece.shape[0]), (3, start, piece.shape[0])]
    return pieces, tuple(offsets)


def per_device(states, inject, final_cotangent, weight, norm_gain):
    micro_count, row_count, dim = inject.shape
    sections = lax.axis_size("section")
    section, shard = lax.axis_index("section"), lax.axis_index("dp")
    own = micro_count * row_count // sections
    place = jnp.stack([section, shard]).astype(jnp.int32)
    gain = norm_gain.reshape(1, dim)
    landed = fetch_weight(weight)

    mine = lax.all_to_all(states[0].reshape(sections, own, dim), "section", 0, 0)
    x, a, q, *a_cut = prepare(place, mine, inject, gain)

    a_ring = jnp.concatenate([a_cut[0]] + [x_move(a_cut[step], step) for step in range(1, X)])
    (low, up), (high, down) = landed[-2:]
    up, down, a_ring = lax.optimization_barrier((up, down, a_ring))
    landed[-2:] = [(low, up), (high, down)]
    pieces, offsets = share_weight(weight, landed)
    a_parts = [a_ring] + [dp_move(a_ring, flip) for flip in (1, 2, 3)]

    g_parts = solve(place, pieces, offsets, a, x, q, gain, final_cotangent, TOLERANCE)

    (a_parts, g_parts) = lax.optimization_barrier((a_parts, g_parts))
    far = jnp.concatenate([dp_move(g_parts[flip], flip) for flip in (1, 2, 3)])
    own_parts = [g_parts[0]] + [x_move(g_parts[0], step) for step in range(1, X)]
    far, own_parts = lax.optimization_barrier((far, own_parts))
    far_parts = [far] + [x_move(far, step) for step in range(1, X)]
    out = block_sum(place, a_parts, own_parts, far_parts)

    got = lax.all_to_all(out, AXES, 0, 0, axis_index_groups=YZ_GROUPS)
    part = dim // 64
    total = jnp.sum(got.astype(f32), axis=0)
    d_weight = total[:part]
    d_gain = total[part + 1 : part + 5].reshape(dim)
    d_inject = got[:, part, : X * own * part].reshape(Y_HI, Z, X, own, part)
    d_inject = jnp.roll(d_inject[:, :, ::-1], (section // Z) % X + 1, axis=2).transpose(0, 2, 1, 3, 4)
    d_inject = d_inject.reshape(micro_count, row_count, part).astype(f32)
    return d_inject, d_weight, d_gain


def solution(mesh):
    in_specs = (
        P("section", None, "dp", None),
        P(None, "dp", None),
        P(None, "dp", None),
        P("dp", None),
        P(),
    )
    out_specs = (P(None, "dp", "section"), P("section", "dp"), P())
    return jax.shard_map(
        per_device, mesh=mesh, in_specs=in_specs, out_specs=out_specs, check_vma=False
    )
```

```python
import functools
import math

import jax
import jax.numpy as jnp
from jax import lax
from jax.experimental import pallas as pl
from jax.experimental.pallas import tpu as pltpu
from jax.sharding import PartitionSpec as P

EPSILON = 1e-06
TOLERANCE = 2.0**-10
LANES = 128
WIDE = 512
AXES = ("section", "dp")
Y_HI, X, Z, Y_LO, CORE = 2, 4, 8, 2, 2
f32, bf16 = jnp.float32, jnp.bfloat16


def own_tokens(ref, section, copies):
    block = ref[section // 4].astype(f32)
    pair = block[0:2]
    for k in range(1, 4):
        pair = jnp.where(section % 4 == k, block[2 * k : 2 * k + 2], pair)
    return jnp.concatenate([pair] * copies, axis=0)


def prepare_kernel(place_ref, states_ref, inject_ref, gain_ref, x_ref, a_ref, q_ref, *cut_refs):
    rows, dim = x_ref.shape
    section = place_ref[0]
    inject = own_tokens(inject_ref, section, 4)
    gain = gain_ref[...]
    groups = rows // 8

    def one(b, _):
        x = jnp.concatenate([states_ref[seg * groups + b].astype(f32) for seg in range(4)], axis=0) + inject
        q = lax.rsqrt(jnp.sum(x * x, axis=1, keepdims=True) * (1.0 / dim) + EPSILON)
        at = pl.ds(pl.multiple_of(b * 8, 8), 8)
        x_ref[at, :] = x
        q_ref[at, :] = jnp.broadcast_to(q, (8, LANES))
        return 0

    lax.fori_loop(0, groups, one, 0)
    a_ref[...] = (x_ref[...] * q_ref[:, 0:1] * gain).astype(bf16)
    eighth = dim // 8
    place = (section // Z) % X
    for cut_ref in cut_refs:
        cut_ref[:, 2 * eighth :] = jnp.zeros((rows, cut_ref.shape[1] - 2 * eighth), bf16)
    for own in range(X):

        @pl.when(place == own)
        def _():
            for step in range(X):
                k = (own + step) % X
                cut_refs[step][:, 0:eighth] = a_ref[:, k * eighth : (k + 1) * eighth]
                cut_refs[step][:, eighth : 2 * eighth] = a_ref[:, dim // 2 + k * eighth : dim // 2 + (k + 1) * eighth]


def prepare(place, states, inject, gain):
    rows, dim = states.shape[0] * states.shape[1], states.shape[2]
    vm = pl.BlockSpec(memory_space=pltpu.VMEM)
    return pl.pallas_call(
        prepare_kernel,
        out_shape=(
            jax.ShapeDtypeStruct((rows, dim), f32),
            jax.ShapeDtypeStruct((rows, dim), bf16),
            jax.ShapeDtypeStruct((rows, LANES), f32),
        )
        + (jax.ShapeDtypeStruct((rows, pl.cdiv(dim // 4, LANES) * LANES), bf16),) * X,
        in_specs=[pl.BlockSpec(memory_space=pltpu.SMEM)] + [vm] * 3,
        out_specs=(vm,) * (3 + X),
        compiler_params=pltpu.CompilerParams(vmem_limit_bytes=32 * 2**20),
        cost_estimate=pl.CostEstimate(flops=20 * 10**9, bytes_accessed=4 * 2**20, transcendentals=0),
    )(place, states, inject, gain)


def solve_kernel(offsets, max_sweeps, tolerance, place_ref, *refs):
    count = len(offsets)
    pieces = refs[:count]
    a_ref, x_ref, q_ref, gain_ref, final_ref = refs[count : count + 5]
    outs = refs[count + 5 : count + 9]
    w, wt, slope, t, p, v, inject_sum, gain_sum, final, sems = refs[count + 9 :]
    rows, dim = x_ref.shape
    section, shard = place_ref[0], place_ref[1]
    small, eighth, groups = dim // 4, dim // 8, rows // 8

    blocks = [(low, min(WIDE, dim - low)) for low in range(0, dim, WIDE)]
    copies = {}
    for m, (low, width) in enumerate(blocks):
        for n, ((flip, start, length), piece) in enumerate(zip(offsets, pieces)):
            at = pl.multiple_of(lax.bitwise_xor(shard, flip) * small + start, 16)
            copies[m, n] = pltpu.make_async_copy(
                piece.at[:, pl.ds(low, width)], w.at[pl.ds(at, length), pl.ds(low, width)], sems.at[m, n]
            )
            copies[m, n].start()
    final[...] = own_tokens(final_ref, section, 4)
    p[...] = jnp.zeros_like(p)
    for m, (low, width) in enumerate(blocks):
        for n in range(count):
            copies[m, n].wait()
        cols = slice(low, low + width)
        h = jnp.dot(a_ref[...], w[:, cols], preferred_element_type=f32)
        s = jax.nn.sigmoid(h)
        sl = s * (1.0 + h * (1.0 - s)) * (1.0 / math.sqrt(max_sweeps))
        slope[:, cols] = sl
        v[:, cols] = (sl * jnp.concatenate([final[:, cols]] * groups, axis=0)).astype(bf16)
        wt[cols, :] = w[:, cols].T
    sub = lax.broadcasted_iota(jnp.int32, (8, LANES), 0)

    def sweep(carry):
        done, _ = carry
        acc = jnp.zeros((rows, LANES), f32)
        for j, width in blocks:
            cols = slice(j, j + width)
            u = jnp.dot(v[...], wt[:, cols], preferred_element_type=f32)
            scaled = u * gain_ref[0:1, cols]
            t[:, cols] = scaled
            scaled = scaled * x_ref[:, cols]
            for k in range(0, width, LANES):
                acc = acc + scaled[:, k : k + LANES]
        q = q_ref[...]
        kappa = q * q * q * (jnp.sum(acc, axis=1, keepdims=True) * (1.0 / dim))

        def columns(n, sums):
            moved, size = sums
            cols = pl.ds(pl.multiple_of(n * LANES, LANES), LANES)
            run, tails = None, [None] * groups
            for b in range(groups - 1, -1, -1):
                at = slice(8 * b, 8 * b + 8)
                new = q[at] * t[at, cols] - kappa[at] * x_ref[at, cols]
                step = new - p[at, cols]
                p[at, cols] = new
                moved = moved + step * step
                run = new if run is None else run + new
                tails[b] = run
            inject_sum[:, cols] = run
            base = final[:, cols]
            for k in (2, 4, 6):
                base = base + jnp.where(sub < 8 - k, pltpu.roll(run, 8 - k, 0), 0.0)
            for b in range(groups):
                at = slice(8 * b, 8 * b + 8)
                c = base if b == groups - 1 else base + tails[b + 1]
                size = size + c * c
                v[at, cols] = (c * slope[at, cols]).astype(bf16)
            return moved, size

        zero = jnp.zeros((8, LANES), f32)
        moved, size = lax.fori_loop(0, dim // LANES, columns, (zero, zero), unroll=3)
        moved = jnp.sum(moved, axis=1, keepdims=True)
        size = jnp.sum(size, axis=1, keepdims=True)
        still = jnp.sum(jnp.where(moved <= size * (tolerance * tolerance), 0.0, 1.0))
        return done + 1, still

    lax.while_loop(
        lambda carry: jnp.logical_and(carry[0] < max_sweeps, carry[1] > 0.0),
        sweep,
        (jnp.int32(0), jnp.float32(1)),
    )

    def finish(n, _):
        cols = pl.ds(pl.multiple_of(n * LANES, LANES), LANES)
        acc = jnp.zeros((8, LANES), f32)
        for b in range(groups):
            at = slice(8 * b, 8 * b + 8)
            acc = acc + q_ref[at] * t[at, cols] * x_ref[at, cols]
        gain_sum[:, cols] = acc / gain_ref[0:1, cols]
        return 0

    lax.fori_loop(0, dim // LANES, finish, 0)
    wide_sub = lax.broadcasted_iota(jnp.int32, (8, small), 0)
    gain_rows = jnp.zeros((8, small), f32)
    total = jnp.sum(gain_sum[...], axis=0, keepdims=True)
    for k in range(4):
        gain_rows = jnp.where(wide_sub == k, total[:, k * small : (k + 1) * small], gain_rows)
    inject_rows = jnp.zeros((8, small), f32)
    total = inject_sum[...]
    total = total + pltpu.roll(total, 4, 0)
    total = total + pltpu.roll(total, 2, 0)
    for k in range(X):
        part = jnp.concatenate(
            [total[:, k * eighth : (k + 1) * eighth], total[:, dim // 2 + k * eighth : dim // 2 + (k + 1) * eighth]],
            axis=1,
        )
        inject_rows = jnp.where(wide_sub // 2 == k, part, inject_rows)
    extra = jnp.concatenate([inject_rows, gain_rows], axis=0).astype(bf16)
    for own in range(4):

        @pl.when(shard == own)
        def _():
            for flip in range(4):
                block = own ^ flip
                outs[flip][0:rows] = v[:, block * small : (block + 1) * small]

    for flip in range(4):
        outs[flip][rows : rows + 16] = extra


def solve(place, pieces, offsets, a, x, q, gain, final, tolerance):
    rows, dim = x.shape
    n = len(pieces)
    vm = pl.BlockSpec(memory_space=pltpu.VMEM)
    return pl.pallas_call(
        functools.partial(solve_kernel, offsets, 64, tolerance),
        out_shape=(jax.ShapeDtypeStruct((rows + 16, dim // 4), bf16),) * 4,
        in_specs=[pl.BlockSpec(memory_space=pltpu.SMEM)] + [pl.BlockSpec(memory_space=pl.ANY)] * n + [vm] * 5,
        out_specs=(vm,) * 4,
        scratch_shapes=[pltpu.VMEM((dim, dim), bf16)] * 2
        + [pltpu.VMEM((rows, dim), f32)] * 3
        + [pltpu.VMEM((rows, dim), bf16)]
        + [pltpu.VMEM((8, dim), f32)] * 3
        + [pltpu.SemaphoreType.DMA((pl.cdiv(dim, WIDE), n))],
        compiler_params=pltpu.CompilerParams(vmem_limit_bytes=56 * 2**20),
        cost_estimate=pl.CostEstimate(flops=4 * 10**10, bytes_accessed=16 * 2**20, transcendentals=0),
    )(place, *pieces, a, x, q, gain, final)


def block_kernel(rows, dim, place_ref, *refs):
    a_refs, own_refs, far_refs = refs[:4], refs[4:8], refs[8:12]
    out_ref, a, g, sems = refs[12:]
    small, part = dim // 4, dim // 64
    tall = rows + 16
    copies = [pltpu.make_async_copy(a_refs[flip], a.at[flip], sems.at[flip]) for flip in range(4)]
    for step in range(X):
        copies.append(pltpu.make_async_copy(own_refs[step], g.at[pl.ds(step * tall, tall)], sems.at[4 + step]))
        copies.append(pltpu.make_async_copy(far_refs[step], g.at[pl.ds((4 + 3 * step) * tall, 3 * tall)], sems.at[8 + step]))
    for copy in copies:
        copy.start()
    for copy in copies:
        copy.wait()

    def slot(flip, step):
        return tall * (step if flip == 0 else 3 + 3 * step + flip)

    places = [(flip, step) for flip in range(4) for step in range(X)]
    left = jnp.concatenate([a[flip, step * rows : (step + 1) * rows] for flip, step in places], axis=0)
    right = jnp.concatenate([g[slot(flip, step) : slot(flip, step) + rows] for flip, step in places], axis=0)
    block = lax.dot_general(left, right, (((0,), (0,)), ((), ())), preferred_element_type=f32)
    gain = jnp.zeros((8, small), f32)
    injects = []
    for flip, step in places:
        extra = g[slot(flip, step) + rows : slot(flip, step) + tall].astype(f32)
        gain = gain + extra[8:16]
        if flip == 0:
            own = extra[0:2]
            for k in range(1, X):
                own = jnp.where((place_ref[0] // Z) % X == k, extra[2 * k : 2 * k + 2], own)
            injects.append(own)
    inject = jnp.concatenate(injects, axis=0)
    for k in range(16):
        line = jnp.concatenate(
            [inject[n : n + 1, k * part : (k + 1) * part] for n in range(8)] + [jnp.zeros((1, small - 8 * part), f32)],
            axis=1,
        )
        out_ref[k] = jnp.concatenate([block[k * part : (k + 1) * part], line, gain[0:5]], axis=0).astype(bf16)


def block_sum(place, a_parts, own_parts, far_parts):
    rows, small = a_parts[0].shape[0] // X, own_parts[0].shape[1]
    hold = pl.BlockSpec(memory_space=pl.ANY)
    return pl.pallas_call(
        functools.partial(block_kernel, rows, 4 * small),
        out_shape=jax.ShapeDtypeStruct((16, 48, small), bf16),
        in_specs=[pl.BlockSpec(memory_space=pltpu.SMEM)] + [hold] * 12,
        out_specs=pl.BlockSpec(memory_space=pltpu.VMEM),
        scratch_shapes=[
            pltpu.VMEM((4,) + a_parts[0].shape, bf16),
            pltpu.VMEM((16 * (rows + 16), small), bf16),
            pltpu.SemaphoreType.DMA((12,)),
        ],
        compiler_params=pltpu.CompilerParams(vmem_limit_bytes=48 * 2**20),
    )(place, *a_parts, *own_parts, *far_parts)


def flat(y, x, z, core):
    return (((y // Y_LO) * X + x) * Z + z) * 4 + (y % Y_LO) * CORE + core


PLACES = [
    (y, x, z, core)
    for y in range(Y_HI * Y_LO)
    for x in range(X)
    for z in range(Z)
    for core in range(CORE)
]


def move(value, target):
    return lax.ppermute(value, AXES, [(flat(*place), flat(*target(*place))) for place in PLACES])


def y_move(value, steps):
    return move(value, lambda y, x, z, core: ((y + steps) % (Y_HI * Y_LO), x, z, core))


def x_move(value, steps):
    return move(value, lambda y, x, z, core: (y, (x + steps) % X, z, core))


def dp_move(value, flip):
    return move(value, lambda y, x, z, core: (y ^ (flip // CORE), x, z, core ^ (flip % CORE)))


YZ_GROUPS = [
    [flat(yh * Y_LO + d // CORE, x, z, d % CORE) for yh in range(Y_HI) for z in range(Z)]
    for x in range(X)
    for d in range(4)
]


def fetch_weight(weight, cut):
    half = weight.shape[0] // 2
    first = y_move(weight[:cut], 1), y_move(weight[half : half + cut], -1)
    source, first = lax.optimization_barrier((weight, first))
    return first, (y_move(source[cut:half], 1), y_move(source[half + cut :], -1))


def per_device(states, inject, final_cotangent, weight, norm_gain):
    micro_count, row_count, dim = inject.shape
    sections = lax.axis_size("section")
    section, shard = lax.axis_index("section"), lax.axis_index("dp")
    own = micro_count * row_count // sections
    place = jnp.stack([section, shard]).astype(jnp.int32)
    gain = norm_gain.reshape(1, dim)
    cut = weight.shape[0] // 84 * 16
    first, second = fetch_weight(weight, cut)

    mine = lax.all_to_all(states[0].reshape(sections, own, dim), "section", 0, 0)
    x, a, q, *a_cut = prepare(place, mine, inject, gain)

    a_ring = jnp.concatenate([a_cut[0]] + [x_move(a_cut[step], step) for step in range(1, X)])
    shared = tuple(dp_move(piece, 1) for piece in first)
    second, shared, a_ring = lax.optimization_barrier((second, shared, a_ring))
    half = weight.shape[0] // 2
    pieces, offsets = [weight, dp_move(weight, 1)], [(0, 0, 2 * half), (1, 0, 2 * half)]
    for start, piece, other in zip((0, half), first, shared):
        pieces += [piece, other]
        offsets += [(2, start, cut), (3, start, cut)]
    for start, piece in zip((cut, half + cut), second):
        pieces += [piece, dp_move(piece, 1)]
        offsets += [(2, start, half - cut), (3, start, half - cut)]
    offsets = tuple(offsets)
    a_parts = [a_ring] + [dp_move(a_ring, flip) for flip in (1, 2, 3)]

    g_parts = solve(place, pieces, offsets, a, x, q, gain, final_cotangent, TOLERANCE)

    (a_parts, g_parts) = lax.optimization_barrier((a_parts, g_parts))
    core_part, chip_part, chip_more = (dp_move(g_parts[flip], flip) for flip in (1, 2, 3))
    own_part, core_part = lax.optimization_barrier((g_parts[0], core_part))
    own_parts = [g_parts[0]] + [x_move(own_part, step) for step in range(1, X)]
    far = jnp.concatenate([core_part, chip_part, chip_more])
    far, own_parts = lax.optimization_barrier((far, own_parts))
    far_parts = [far] + [x_move(far, step) for step in range(1, X)]
    out = block_sum(place, a_parts, own_parts, far_parts)

    got = lax.all_to_all(out, AXES, 0, 0, axis_index_groups=YZ_GROUPS)
    part = dim // 64
    total = jnp.sum(got.astype(f32), axis=0)
    d_weight = total[:part]
    d_gain = total[part + 1 : part + 5].reshape(dim)
    d_inject = got[:, part, : X * own * part].reshape(Y_HI, Z, X, own, part)
    d_inject = jnp.roll(d_inject[:, :, ::-1], (section // Z) % X + 1, axis=2).transpose(0, 2, 1, 3, 4)
    d_inject = d_inject.reshape(micro_count, row_count, part).astype(f32)
    return d_inject, d_weight, d_gain


def solution(mesh):
    in_specs = (
        P("section", None, "dp", None),
        P(None, "dp", None),
        P(None, "dp", None),
        P("dp", None),
        P(),
    )
    out_specs = (P(None, "dp", "section"), P("section", "dp"), P())
    return jax.shard_map(
        per_device, mesh=mesh, in_specs=in_specs, out_specs=out_specs, check_vma=False
    )
```

```python
import functools
import math

import jax
import jax.numpy as jnp
from jax import lax
from jax.experimental import pallas as pl
from jax.experimental.pallas import tpu as pltpu
from jax.sharding import PartitionSpec as P

EPSILON = 1e-06
TOLERANCE = 2.0**-10
LANES = 128
HALVES = (64, 224)
WIDE = 512
AXES = ("section", "dp")
Y_HI, X, Z, Y_LO, CORE = 2, 4, 8, 2, 2
f32, bf16 = jnp.float32, jnp.bfloat16


def own_tokens(ref, section, copies):
    block = ref[section // 4].astype(f32)
    pair = block[0:2]
    for k in range(1, 4):
        pair = jnp.where(section % 4 == k, block[2 * k : 2 * k + 2], pair)
    return jnp.concatenate([pair] * copies, axis=0)


def prepare_kernel(place_ref, states_ref, inject_ref, gain_ref, x_ref, a_ref, q_ref, *cut_refs):
    rows, dim = x_ref.shape
    section = place_ref[0]
    inject = own_tokens(inject_ref, section, 4)
    gain = gain_ref[...]
    groups = rows // 8

    def one(b, _):
        x = jnp.concatenate([states_ref[seg * groups + b].astype(f32) for seg in range(4)], axis=0) + inject
        q = lax.rsqrt(jnp.sum(x * x, axis=1, keepdims=True) * (1.0 / dim) + EPSILON)
        at = pl.ds(pl.multiple_of(b * 8, 8), 8)
        x_ref[at, :] = x
        q_ref[at, :] = jnp.broadcast_to(q, (8, LANES))
        return 0

    lax.fori_loop(0, groups, one, 0)
    a_ref[...] = (x_ref[...] * q_ref[:, 0:1] * gain).astype(bf16)
    eighth = dim // 8
    place = (section // Z) % X
    for cut_ref in cut_refs:
        cut_ref[:, 2 * eighth :] = jnp.zeros((rows, cut_ref.shape[1] - 2 * eighth), bf16)
    for own in range(X):

        @pl.when(place == own)
        def _():
            for step in range(X):
                k = (own + step) % X
                cut_refs[step][:, 0:eighth] = a_ref[:, k * eighth : (k + 1) * eighth]
                cut_refs[step][:, eighth : 2 * eighth] = a_ref[:, dim // 2 + k * eighth : dim // 2 + (k + 1) * eighth]


def prepare(place, states, inject, gain):
    rows, dim = states.shape[0] * states.shape[1], states.shape[2]
    vm = pl.BlockSpec(memory_space=pltpu.VMEM)
    return pl.pallas_call(
        prepare_kernel,
        out_shape=(
            jax.ShapeDtypeStruct((rows, dim), f32),
            jax.ShapeDtypeStruct((rows, dim), bf16),
            jax.ShapeDtypeStruct((rows, LANES), f32),
        )
        + (jax.ShapeDtypeStruct((rows, pl.cdiv(dim // 4, LANES) * LANES), bf16),) * X,
        in_specs=[pl.BlockSpec(memory_space=pltpu.SMEM)] + [vm] * 3,
        out_specs=(vm,) * (3 + X),
        compiler_params=pltpu.CompilerParams(vmem_limit_bytes=32 * 2**20),
        cost_estimate=pl.CostEstimate(flops=20 * 10**9, bytes_accessed=4 * 2**20, transcendentals=0),
    )(place, states, inject, gain)


def solve_kernel(offsets, max_sweeps, tolerance, place_ref, *refs):
    count = len(offsets)
    pieces = refs[:count]
    a_ref, x_ref, q_ref, gain_ref, final_ref = refs[count : count + 5]
    outs = refs[count + 5 : count + 9]
    w, wt, slope, t, p, v, inject_sum, gain_sum, final, sems = refs[count + 9 :]
    rows, dim = x_ref.shape
    section, shard = place_ref[0], place_ref[1]
    small, eighth, groups = dim // 4, dim // 8, rows // 8

    blocks = [(low, min(WIDE, dim - low)) for low in range(0, dim, WIDE)]
    copies = {}
    for m, (low, width) in enumerate(blocks):
        for n, ((flip, start, length), piece) in enumerate(zip(offsets, pieces)):
            at = pl.multiple_of(lax.bitwise_xor(shard, flip) * small + start, 16)
            copies[m, n] = pltpu.make_async_copy(
                piece.at[:, pl.ds(low, width)], w.at[pl.ds(at, length), pl.ds(low, width)], sems.at[m, n]
            )
            copies[m, n].start()
    final[...] = own_tokens(final_ref, section, 4)
    p[...] = jnp.zeros_like(p)
    for m, (low, width) in enumerate(blocks):
        for n in range(count):
            copies[m, n].wait()
        cols = slice(low, low + width)
        h = jnp.dot(a_ref[...], w[:, cols], preferred_element_type=f32)
        s = jax.nn.sigmoid(h)
        sl = s * (1.0 + h * (1.0 - s)) * (1.0 / math.sqrt(max_sweeps))
        slope[:, cols] = sl
        v[:, cols] = (sl * jnp.concatenate([final[:, cols]] * groups, axis=0)).astype(bf16)
        wt[cols, :] = w[:, cols].T
    sub = lax.broadcasted_iota(jnp.int32, (8, LANES), 0)

    def sweep(carry):
        done, _ = carry
        acc = jnp.zeros((rows, LANES), f32)
        for j, width in blocks:
            cols = slice(j, j + width)
            u = jnp.dot(v[...], wt[:, cols], preferred_element_type=f32)
            scaled = u * gain_ref[0:1, cols]
            t[:, cols] = scaled
            scaled = scaled * x_ref[:, cols]
            for k in range(0, width, LANES):
                acc = acc + scaled[:, k : k + LANES]
        q = q_ref[...]
        kappa = q * q * q * (jnp.sum(acc, axis=1, keepdims=True) * (1.0 / dim))

        def columns(n, sums):
            moved, size = sums
            cols = pl.ds(pl.multiple_of(n * LANES, LANES), LANES)
            run, tails = None, [None] * groups
            for b in range(groups - 1, -1, -1):
                at = slice(8 * b, 8 * b + 8)
                new = q[at] * t[at, cols] - kappa[at] * x_ref[at, cols]
                step = new - p[at, cols]
                p[at, cols] = new
                moved = moved + step * step
                run = new if run is None else run + new
                tails[b] = run
            inject_sum[:, cols] = run
            base = final[:, cols]
            for k in (2, 4, 6):
                base = base + jnp.where(sub < 8 - k, pltpu.roll(run, 8 - k, 0), 0.0)
            for b in range(groups):
                at = slice(8 * b, 8 * b + 8)
                c = base if b == groups - 1 else base + tails[b + 1]
                size = size + c * c
                v[at, cols] = (c * slope[at, cols]).astype(bf16)
            return moved, size

        zero = jnp.zeros((8, LANES), f32)
        moved, size = lax.fori_loop(0, dim // LANES, columns, (zero, zero), unroll=3)
        moved = jnp.sum(moved, axis=1, keepdims=True)
        size = jnp.sum(size, axis=1, keepdims=True)
        still = jnp.sum(jnp.where(moved <= size * (tolerance * tolerance), 0.0, 1.0))
        return done + 1, still

    lax.while_loop(
        lambda carry: jnp.logical_and(carry[0] < max_sweeps, carry[1] > 0.0),
        sweep,
        (jnp.int32(0), jnp.float32(1)),
    )

    def finish(n, _):
        cols = pl.ds(pl.multiple_of(n * LANES, LANES), LANES)
        acc = jnp.zeros((8, LANES), f32)
        for b in range(groups):
            at = slice(8 * b, 8 * b + 8)
            acc = acc + q_ref[at] * t[at, cols] * x_ref[at, cols]
        gain_sum[:, cols] = acc / gain_ref[0:1, cols]
        return 0

    lax.fori_loop(0, dim // LANES, finish, 0)
    wide_sub = lax.broadcasted_iota(jnp.int32, (8, small), 0)
    gain_rows = jnp.zeros((8, small), f32)
    total = jnp.sum(gain_sum[...], axis=0, keepdims=True)
    for k in range(4):
        gain_rows = jnp.where(wide_sub == k, total[:, k * small : (k + 1) * small], gain_rows)
    inject_rows = jnp.zeros((8, small), f32)
    total = inject_sum[...]
    total = total + pltpu.roll(total, 4, 0)
    total = total + pltpu.roll(total, 2, 0)
    for k in range(X):
        part = jnp.concatenate(
            [total[:, k * eighth : (k + 1) * eighth], total[:, dim // 2 + k * eighth : dim // 2 + (k + 1) * eighth]],
            axis=1,
        )
        inject_rows = jnp.where(wide_sub // 2 == k, part, inject_rows)
    extra = jnp.concatenate([inject_rows, gain_rows], axis=0).astype(bf16)
    for own in range(4):

        @pl.when(shard == own)
        def _():
            for flip in range(4):
                block = own ^ flip
                outs[flip][0:rows] = v[:, block * small : (block + 1) * small]

    for flip in range(4):
        outs[flip][rows : rows + 16] = extra


def solve(place, pieces, offsets, a, x, q, gain, final, tolerance):
    rows, dim = x.shape
    n = len(pieces)
    vm = pl.BlockSpec(memory_space=pltpu.VMEM)
    return pl.pallas_call(
        functools.partial(solve_kernel, offsets, 64, tolerance),
        out_shape=(jax.ShapeDtypeStruct((rows + 16, dim // 4), bf16),) * 4,
        in_specs=[pl.BlockSpec(memory_space=pltpu.SMEM)] + [pl.BlockSpec(memory_space=pl.ANY)] * n + [vm] * 5,
        out_specs=(vm,) * 4,
        scratch_shapes=[pltpu.VMEM((dim, dim), bf16)] * 2
        + [pltpu.VMEM((rows, dim), f32)] * 3
        + [pltpu.VMEM((rows, dim), bf16)]
        + [pltpu.VMEM((8, dim), f32)] * 3
        + [pltpu.SemaphoreType.DMA((pl.cdiv(dim, WIDE), n))],
        compiler_params=pltpu.CompilerParams(vmem_limit_bytes=56 * 2**20),
        cost_estimate=pl.CostEstimate(flops=4 * 10**10, bytes_accessed=16 * 2**20, transcendentals=0),
    )(place, *pieces, a, x, q, gain, final)


def block_kernel(rows, dim, place_ref, *refs):
    a_refs, own_refs, far_refs, half_refs = refs[:4], refs[4:7], refs[7:10], refs[10:12]
    out_ref, a, g, sems = refs[12:]
    small, part = dim // 4, dim // 64
    tall = rows + 16
    copies = [pltpu.make_async_copy(a_refs[flip], a.at[flip], sems.at[flip]) for flip in range(4)]
    for n, step in enumerate((0, 1, 3)):
        copies.append(pltpu.make_async_copy(own_refs[n], g.at[pl.ds(step * tall, tall)], sems.at[4 + n]))
        copies.append(pltpu.make_async_copy(far_refs[n], g.at[pl.ds((4 + 3 * step) * tall, 3 * tall)], sems.at[7 + n]))
    own_cut, far_cut = HALVES
    first, last = half_refs
    for n, (ref, start, length, at) in enumerate(
        (
            (first, 0, own_cut, 2 * tall),
            (first, own_cut, far_cut, 10 * tall),
            (last, 0, tall - own_cut, 2 * tall + own_cut),
            (last, tall - own_cut, 3 * tall - far_cut, 10 * tall + far_cut),
        )
    ):
        copies.append(pltpu.make_async_copy(ref.at[pl.ds(start, length)], g.at[pl.ds(at, length)], sems.at[10 + n]))
    for copy in copies:
        copy.start()
    for copy in copies:
        copy.wait()

    def slot(flip, step):
        return tall * (step if flip == 0 else 3 + 3 * step + flip)

    places = [(flip, step) for flip in range(4) for step in range(X)]
    left = jnp.concatenate([a[flip, step * rows : (step + 1) * rows] for flip, step in places], axis=0)
    right = jnp.concatenate([g[slot(flip, step) : slot(flip, step) + rows] for flip, step in places], axis=0)
    block = lax.dot_general(left, right, (((0,), (0,)), ((), ())), preferred_element_type=f32)
    gain = jnp.zeros((8, small), f32)
    injects = []
    for flip, step in places:
        extra = g[slot(flip, step) + rows : slot(flip, step) + tall].astype(f32)
        gain = gain + extra[8:16]
        if flip == 0:
            own = extra[0:2]
            for k in range(1, X):
                own = jnp.where((place_ref[0] // Z) % X == k, extra[2 * k : 2 * k + 2], own)
            injects.append(own)
    inject = jnp.concatenate(injects, axis=0)
    for k in range(16):
        line = jnp.concatenate(
            [inject[n : n + 1, k * part : (k + 1) * part] for n in range(8)] + [jnp.zeros((1, small - 8 * part), f32)],
            axis=1,
        )
        out_ref[k] = jnp.concatenate([block[k * part : (k + 1) * part], line, gain[0:5]], axis=0).astype(bf16)


def block_sum(place, a_parts, own_parts, far_parts, halves):
    rows, small = a_parts[0].shape[0] // X, own_parts[0].shape[1]
    hold = pl.BlockSpec(memory_space=pl.ANY)
    return pl.pallas_call(
        functools.partial(block_kernel, rows, 4 * small),
        out_shape=jax.ShapeDtypeStruct((16, 48, small), bf16),
        in_specs=[pl.BlockSpec(memory_space=pltpu.SMEM)] + [hold] * 12,
        out_specs=pl.BlockSpec(memory_space=pltpu.VMEM),
        scratch_shapes=[
            pltpu.VMEM((4,) + a_parts[0].shape, bf16),
            pltpu.VMEM((16 * (rows + 16), small), bf16),
            pltpu.SemaphoreType.DMA((14,)),
        ],
        compiler_params=pltpu.CompilerParams(vmem_limit_bytes=48 * 2**20),
    )(place, *a_parts, *own_parts, *far_parts, *halves)


def flat(y, x, z, core):
    return (((y // Y_LO) * X + x) * Z + z) * 4 + (y % Y_LO) * CORE + core


PLACES = [
    (y, x, z, core)
    for y in range(Y_HI * Y_LO)
    for x in range(X)
    for z in range(Z)
    for core in range(CORE)
]


def move(value, target):
    return lax.ppermute(value, AXES, [(flat(*place), flat(*target(*place))) for place in PLACES])


def y_move(value, steps):
    return move(value, lambda y, x, z, core: ((y + steps) % (Y_HI * Y_LO), x, z, core))


def x_move(value, steps):
    return move(value, lambda y, x, z, core: (y, (x + steps) % X, z, core))


def dp_move(value, flip):
    return move(value, lambda y, x, z, core: (y ^ (flip // CORE), x, z, core ^ (flip % CORE)))


YZ_GROUPS = [
    [flat(yh * Y_LO + d // CORE, x, z, d % CORE) for yh in range(Y_HI) for z in range(Z)]
    for x in range(X)
    for d in range(4)
]


def fetch_weight(weight, cut):
    half = weight.shape[0] // 2
    first = y_move(weight[:cut], 1), y_move(weight[half : half + cut], -1)
    source, first = lax.optimization_barrier((weight, first))
    return first, (y_move(source[cut:half], 1), y_move(source[half + cut :], -1))


def per_device(states, inject, final_cotangent, weight, norm_gain):
    micro_count, row_count, dim = inject.shape
    sections = lax.axis_size("section")
    section, shard = lax.axis_index("section"), lax.axis_index("dp")
    own = micro_count * row_count // sections
    place = jnp.stack([section, shard]).astype(jnp.int32)
    gain = norm_gain.reshape(1, dim)
    cut = weight.shape[0] // 84 * 16
    first, second = fetch_weight(weight, cut)

    mine = lax.all_to_all(states[0].reshape(sections, own, dim), "section", 0, 0)
    x, a, q, *a_cut = prepare(place, mine, inject, gain)

    a_ring = jnp.concatenate([a_cut[0]] + [x_move(a_cut[step], step) for step in range(1, X)])
    shared = tuple(dp_move(piece, 1) for piece in first)
    second, shared, a_ring = lax.optimization_barrier((second, shared, a_ring))
    half = weight.shape[0] // 2
    pieces, offsets = [weight, dp_move(weight, 1)], [(0, 0, 2 * half), (1, 0, 2 * half)]
    for start, piece, other in zip((0, half), first, shared):
        pieces += [piece, other]
        offsets += [(2, start, cut), (3, start, cut)]
    for start, piece in zip((cut, half + cut), second):
        pieces += [piece, dp_move(piece, 1)]
        offsets += [(2, start, half - cut), (3, start, half - cut)]
    offsets = tuple(offsets)
    a_parts = [a_ring] + [dp_move(a_ring, flip) for flip in (1, 2, 3)]

    g_parts = solve(place, pieces, offsets, a, x, q, gain, final_cotangent, TOLERANCE)

    (a_parts, g_parts) = lax.optimization_barrier((a_parts, g_parts))
    core_part, chip_part, chip_more = (dp_move(g_parts[flip], flip) for flip in (1, 2, 3))
    own_part, core_part = lax.optimization_barrier((g_parts[0], core_part))
    own_parts = [g_parts[0], x_move(own_part, 1), x_move(own_part, -1)]
    far = jnp.concatenate([core_part, chip_part, chip_more])
    far, own_parts = lax.optimization_barrier((far, own_parts))
    far_parts = [far, x_move(far, 1), x_move(far, -1)]
    own_cut, far_cut = HALVES
    halves = [
        x_move(jnp.concatenate([own_parts[1][:own_cut], far_parts[1][:far_cut]]), 1),
        x_move(jnp.concatenate([own_parts[2][own_cut:], far_parts[2][far_cut:]]), -1),
    ]
    out = block_sum(place, a_parts, own_parts, far_parts, halves)

    got = lax.all_to_all(out, AXES, 0, 0, axis_index_groups=YZ_GROUPS)
    part = dim // 64
    total = jnp.sum(got.astype(f32), axis=0)
    d_weight = total[:part]
    d_gain = total[part + 1 : part + 5].reshape(dim)
    d_inject = got[:, part, : X * own * part].reshape(Y_HI, Z, X, own, part)
    d_inject = jnp.roll(d_inject[:, :, ::-1], (section // Z) % X + 1, axis=2).transpose(0, 2, 1, 3, 4)
    d_inject = d_inject.reshape(micro_count, row_count, part).astype(f32)
    return d_inject, d_weight, d_gain


def solution(mesh):
    in_specs = (
        P("section", None, "dp", None),
        P(None, "dp", None),
        P(None, "dp", None),
        P("dp", None),
        P(),
    )
    out_specs = (P(None, "dp", "section"), P("section", "dp"), P())
    return jax.shard_map(
        per_device, mesh=mesh, in_specs=in_specs, out_specs=out_specs, check_vma=False
    )
```

```python
import functools
import math

import jax
import jax.numpy as jnp
from jax import lax
from jax.experimental import pallas as pl
from jax.experimental.pallas import tpu as pltpu
from jax.sharding import PartitionSpec as P

EPSILON = 1e-06
TOLERANCE = 2.0**-10
LANES = 128
HALVES = (64, 224)
WIDE = 512
AXES = ("section", "dp")
Y_HI, X, Z, Y_LO, CORE = 2, 4, 8, 2, 2
f32, bf16 = jnp.float32, jnp.bfloat16


def own_tokens(ref, section, copies):
    block = ref[section // 4].astype(f32)
    pair = block[0:2]
    for k in range(1, 4):
        pair = jnp.where(section % 4 == k, block[2 * k : 2 * k + 2], pair)
    return jnp.concatenate([pair] * copies, axis=0)


def prepare_kernel(place_ref, states_ref, inject_ref, gain_ref, x_ref, a_ref, q_ref, *cut_refs):
    rows, dim = x_ref.shape
    section = place_ref[0]
    inject = own_tokens(inject_ref, section, 4)
    gain = gain_ref[...]
    groups = rows // 8

    def one(b, _):
        x = jnp.concatenate([states_ref[seg * groups + b].astype(f32) for seg in range(4)], axis=0) + inject
        q = lax.rsqrt(jnp.sum(x * x, axis=1, keepdims=True) * (1.0 / dim) + EPSILON)
        at = pl.ds(pl.multiple_of(b * 8, 8), 8)
        x_ref[at, :] = x
        q_ref[at, :] = jnp.broadcast_to(q, (8, LANES))
        return 0

    lax.fori_loop(0, groups, one, 0)
    a_ref[...] = (x_ref[...] * q_ref[:, 0:1] * gain).astype(bf16)
    eighth = dim // 8
    place = (section // Z) % X
    for cut_ref in cut_refs:
        cut_ref[:, 2 * eighth :] = jnp.zeros((rows, cut_ref.shape[1] - 2 * eighth), bf16)
    for own in range(X):

        @pl.when(place == own)
        def _():
            for step in range(X):
                k = (own + step) % X
                cut_refs[step][:, 0:eighth] = a_ref[:, k * eighth : (k + 1) * eighth]
                cut_refs[step][:, eighth : 2 * eighth] = a_ref[:, dim // 2 + k * eighth : dim // 2 + (k + 1) * eighth]


def prepare(place, states, inject, gain):
    rows, dim = states.shape[0] * states.shape[1], states.shape[2]
    vm = pl.BlockSpec(memory_space=pltpu.VMEM)
    return pl.pallas_call(
        prepare_kernel,
        out_shape=(
            jax.ShapeDtypeStruct((rows, dim), f32),
            jax.ShapeDtypeStruct((rows, dim), bf16),
            jax.ShapeDtypeStruct((rows, LANES), f32),
        )
        + (jax.ShapeDtypeStruct((rows, pl.cdiv(dim // 4, LANES) * LANES), bf16),) * X,
        in_specs=[pl.BlockSpec(memory_space=pltpu.SMEM)] + [vm] * 3,
        out_specs=(vm,) * (3 + X),
        compiler_params=pltpu.CompilerParams(vmem_limit_bytes=32 * 2**20),
        cost_estimate=pl.CostEstimate(flops=20 * 10**9, bytes_accessed=4 * 2**20, transcendentals=0),
    )(place, states, inject, gain)


def solve_kernel(offsets, max_sweeps, tolerance, place_ref, *refs):
    count = len(offsets)
    pieces = refs[:count]
    a_ref, x_ref, q_ref, gain_ref, final_ref = refs[count : count + 5]
    outs = refs[count + 5 : count + 9]
    w, wt, slope, t, p, v, inject_sum, gain_sum, final, sems = refs[count + 9 :]
    rows, dim = x_ref.shape
    section, shard = place_ref[0], place_ref[1]
    small, eighth, groups = dim // 4, dim // 8, rows // 8

    blocks = [(low, min(WIDE, dim - low)) for low in range(0, dim, WIDE)]
    copies = {}
    for m, (low, width) in enumerate(blocks):
        for n, ((flip, start, length), piece) in enumerate(zip(offsets, pieces)):
            at = pl.multiple_of(lax.bitwise_xor(shard, flip) * small + start, 16)
            copies[m, n] = pltpu.make_async_copy(
                piece.at[:, pl.ds(low, width)], w.at[pl.ds(at, length), pl.ds(low, width)], sems.at[m, n]
            )
            copies[m, n].start()
    final[...] = own_tokens(final_ref, section, 4)
    p[...] = jnp.zeros_like(p)
    for m, (low, width) in enumerate(blocks):
        for n in range(count):
            copies[m, n].wait()
        cols = slice(low, low + width)
        h = jnp.dot(a_ref[...], w[:, cols], preferred_element_type=f32)
        s = jax.nn.sigmoid(h)
        sl = s * (1.0 + h * (1.0 - s)) * (1.0 / math.sqrt(max_sweeps))
        slope[:, cols] = sl
        v[:, cols] = (sl * jnp.concatenate([final[:, cols]] * groups, axis=0)).astype(bf16)
        wt[cols, :] = w[:, cols].T
    sub = lax.broadcasted_iota(jnp.int32, (8, LANES), 0)

    def sweep(carry):
        done, _ = carry
        acc = jnp.zeros((rows, LANES), f32)
        for j, width in blocks:
            cols = slice(j, j + width)
            u = jnp.dot(v[...], wt[:, cols], preferred_element_type=f32)
            scaled = u * gain_ref[0:1, cols]
            t[:, cols] = scaled
            scaled = scaled * x_ref[:, cols]
            for k in range(0, width, LANES):
                acc = acc + scaled[:, k : k + LANES]
        q = q_ref[...]
        kappa = q * q * q * (jnp.sum(acc, axis=1, keepdims=True) * (1.0 / dim))

        def columns(n, sums):
            moved, size = sums
            cols = pl.ds(pl.multiple_of(n * LANES, LANES), LANES)
            run, tails = None, [None] * groups
            for b in range(groups - 1, -1, -1):
                at = slice(8 * b, 8 * b + 8)
                new = q[at] * t[at, cols] - kappa[at] * x_ref[at, cols]
                step = new - p[at, cols]
                p[at, cols] = new
                moved = moved + step * step
                run = new if run is None else run + new
                tails[b] = run
            inject_sum[:, cols] = run
            base = final[:, cols]
            for k in (2, 4, 6):
                base = base + jnp.where(sub < 8 - k, pltpu.roll(run, 8 - k, 0), 0.0)
            for b in range(groups):
                at = slice(8 * b, 8 * b + 8)
                c = base if b == groups - 1 else base + tails[b + 1]
                size = size + c * c
                v[at, cols] = (c * slope[at, cols]).astype(bf16)
            return moved, size

        zero = jnp.zeros((8, LANES), f32)
        moved, size = lax.fori_loop(0, dim // LANES, columns, (zero, zero), unroll=3)
        moved = jnp.sum(moved, axis=1, keepdims=True)
        size = jnp.sum(size, axis=1, keepdims=True)
        still = jnp.sum(jnp.where(moved <= size * (tolerance * tolerance), 0.0, 1.0))
        return done + 1, still

    lax.while_loop(
        lambda carry: jnp.logical_and(carry[0] < max_sweeps, carry[1] > 0.0),
        sweep,
        (jnp.int32(0), jnp.float32(1)),
    )

    def finish(n, _):
        cols = pl.ds(pl.multiple_of(n * LANES, LANES), LANES)
        acc = jnp.zeros((8, LANES), f32)
        for b in range(groups):
            at = slice(8 * b, 8 * b + 8)
            acc = acc + q_ref[at] * t[at, cols] * x_ref[at, cols]
        gain_sum[:, cols] = acc / gain_ref[0:1, cols]
        return 0

    lax.fori_loop(0, dim // LANES, finish, 0)
    wide_sub = lax.broadcasted_iota(jnp.int32, (8, small), 0)
    gain_rows = jnp.zeros((8, small), f32)
    total = jnp.sum(gain_sum[...], axis=0, keepdims=True)
    for k in range(4):
        gain_rows = jnp.where(wide_sub == k, total[:, k * small : (k + 1) * small], gain_rows)
    inject_rows = jnp.zeros((8, small), f32)
    total = inject_sum[...]
    total = total + pltpu.roll(total, 4, 0)
    total = total + pltpu.roll(total, 2, 0)
    for k in range(X):
        part = jnp.concatenate(
            [total[:, k * eighth : (k + 1) * eighth], total[:, dim // 2 + k * eighth : dim // 2 + (k + 1) * eighth]],
            axis=1,
        )
        inject_rows = jnp.where(wide_sub // 2 == k, part, inject_rows)
    extra = jnp.concatenate([inject_rows, gain_rows], axis=0).astype(bf16)
    for own in range(4):

        @pl.when(shard == own)
        def _():
            for flip in range(4):
                block = own ^ flip
                outs[flip][0:rows] = v[:, block * small : (block + 1) * small]

    for flip in range(4):
        outs[flip][rows : rows + 16] = extra


def solve(place, pieces, offsets, a, x, q, gain, final, tolerance):
    rows, dim = x.shape
    n = len(pieces)
    vm = pl.BlockSpec(memory_space=pltpu.VMEM)
    return pl.pallas_call(
        functools.partial(solve_kernel, offsets, 64, tolerance),
        out_shape=(jax.ShapeDtypeStruct((rows + 16, dim // 4), bf16),) * 4,
        in_specs=[pl.BlockSpec(memory_space=pltpu.SMEM)] + [pl.BlockSpec(memory_space=pl.ANY)] * n + [vm] * 5,
        out_specs=(vm,) * 4,
        scratch_shapes=[pltpu.VMEM((dim, dim), bf16)] * 2
        + [pltpu.VMEM((rows, dim), f32)] * 3
        + [pltpu.VMEM((rows, dim), bf16)]
        + [pltpu.VMEM((8, dim), f32)] * 3
        + [pltpu.SemaphoreType.DMA((pl.cdiv(dim, WIDE), n))],
        compiler_params=pltpu.CompilerParams(vmem_limit_bytes=56 * 2**20),
        cost_estimate=pl.CostEstimate(flops=4 * 10**10, bytes_accessed=16 * 2**20, transcendentals=0),
    )(place, *pieces, a, x, q, gain, final)


def own_lines(place_ref, extra):
    lines = extra[0:2]
    for k in range(1, X):
        lines = jnp.where((place_ref[0] // Z) % X == k, extra[2 * k : 2 * k + 2], lines)
    return lines


def near_kernel(rows, steps, place_ref, *refs):
    count = len(steps)
    a_refs, own_refs, far_refs = refs[:4], refs[4 : 4 + count], refs[4 + count : 4 + 2 * count]
    block_ref, gain_ref, inject_ref, a, g, sems = refs[4 + 2 * count :]
    tall = rows + 16
    copies = [pltpu.make_async_copy(a_refs[flip], a.at[flip], sems.at[flip]) for flip in range(4)]
    for n in range(count):
        copies.append(pltpu.make_async_copy(own_refs[n], g.at[pl.ds(4 * n * tall, tall)], sems.at[4 + n]))
        far = g.at[pl.ds((4 * n + 1) * tall, 3 * tall)]
        copies.append(pltpu.make_async_copy(far_refs[n], far, sems.at[4 + count + n]))
    for copy in copies:
        copy.start()
    for copy in copies:
        copy.wait()
    places = [(n, step, flip) for n, step in enumerate(steps) for flip in range(4)]
    left = jnp.concatenate([a[flip, step * rows : (step + 1) * rows] for _, step, flip in places], axis=0)
    starts = [(4 * n + flip) * tall for n, _, flip in places]
    right = jnp.concatenate([g[start : start + rows] for start in starts], axis=0)
    block_ref[...] = lax.dot_general(left, right, (((0,), (0,)), ((), ())), preferred_element_type=f32)
    gain, injects = jnp.zeros(gain_ref.shape, f32), []
    for (_, _, flip), start in zip(places, starts):
        extra = g[start + rows : start + tall].astype(f32)
        gain = gain + extra[8:16]
        if flip == 0:
            injects.append(own_lines(place_ref, extra))
    gain_ref[...] = gain
    inject_ref[...] = jnp.concatenate(injects + [jnp.zeros_like(injects[0])], axis=0)


def block_kernel(rows, dim, place_ref, *refs):
    a_refs, (first, last), (near_ref, gain_ref, inject_ref) = refs[:4], refs[4:6], refs[6:9]
    out_ref, a, g, sems = refs[9:]
    small, part = dim // 4, dim // 64
    tall = rows + 16
    copies = [
        pltpu.make_async_copy(a_refs[flip].at[pl.ds(2 * rows, rows)], a.at[pl.ds(flip * rows, rows)], sems.at[flip])
        for flip in range(4)
    ]
    own_cut, far_cut = HALVES
    for n, (ref, start, length, at) in enumerate(
        (
            (first, 0, own_cut, 0),
            (first, own_cut, far_cut, tall),
            (last, 0, tall - own_cut, own_cut),
            (last, tall - own_cut, 3 * tall - far_cut, tall + far_cut),
        )
    ):
        copies.append(pltpu.make_async_copy(ref.at[pl.ds(start, length)], g.at[pl.ds(at, length)], sems.at[4 + n]))
    for copy in copies:
        copy.start()
    for copy in copies:
        copy.wait()
    right = jnp.concatenate([g[flip * tall : flip * tall + rows] for flip in range(4)], axis=0)
    block = lax.dot_general(a[...], right, (((0,), (0,)), ((), ())), preferred_element_type=f32) + near_ref[...]
    extras = [g[flip * tall + rows : (flip + 1) * tall].astype(f32) for flip in range(4)]
    gain = gain_ref[...] + extras[0][8:16] + extras[1][8:16] + extras[2][8:16] + extras[3][8:16]
    inject = inject_ref[...]
    inject = jnp.concatenate([inject[0:4], own_lines(place_ref, extras[0]), inject[4:6]], axis=0)
    for k in range(16):
        line = jnp.concatenate(
            [inject[n : n + 1, k * part : (k + 1) * part] for n in range(8)] + [jnp.zeros((1, small - 8 * part), f32)],
            axis=1,
        )
        out_ref[k] = jnp.concatenate([block[k * part : (k + 1) * part], line, gain[0:5]], axis=0).astype(bf16)


def near_sum(place, a_parts, own_parts, far_parts):
    steps = (0, 1, 3)
    (deep, wide), (tall, small) = a_parts[0].shape, own_parts[0].shape
    hold, vm = pl.BlockSpec(memory_space=pl.ANY), pl.BlockSpec(memory_space=pltpu.VMEM)
    return pl.pallas_call(
        functools.partial(near_kernel, deep // X, steps),
        out_shape=(
            jax.ShapeDtypeStruct((wide, small), f32),
            jax.ShapeDtypeStruct((8, small), f32),
            jax.ShapeDtypeStruct((8, small), f32),
        ),
        in_specs=[pl.BlockSpec(memory_space=pltpu.SMEM)] + [hold] * 10,
        out_specs=(vm,) * 3,
        scratch_shapes=[
            pltpu.VMEM((4, deep, wide), bf16),
            pltpu.VMEM((12 * tall, small), bf16),
            pltpu.SemaphoreType.DMA((10,)),
        ],
        compiler_params=pltpu.CompilerParams(vmem_limit_bytes=40 * 2**20),
        cost_estimate=pl.CostEstimate(flops=5 * 10**9, bytes_accessed=6 * 2**20, transcendentals=0),
    )(place, *a_parts, *own_parts, *far_parts)


def block_sum(place, a_parts, halves, near):
    (deep, wide), small = a_parts[0].shape, halves[0].shape[1]
    rows = deep // X
    hold, vm = pl.BlockSpec(memory_space=pl.ANY), pl.BlockSpec(memory_space=pltpu.VMEM)
    return pl.pallas_call(
        functools.partial(block_kernel, rows, 4 * small),
        out_shape=jax.ShapeDtypeStruct((16, 48, small), bf16),
        in_specs=[pl.BlockSpec(memory_space=pltpu.SMEM)] + [hold] * 6 + [vm] * 3,
        out_specs=vm,
        scratch_shapes=[
            pltpu.VMEM((4 * rows, wide), bf16),
            pltpu.VMEM((4 * (rows + 16), small), bf16),
            pltpu.SemaphoreType.DMA((8,)),
        ],
        compiler_params=pltpu.CompilerParams(vmem_limit_bytes=40 * 2**20),
    )(place, *a_parts, *halves, *near)


def flat(y, x, z, core):
    return (((y // Y_LO) * X + x) * Z + z) * 4 + (y % Y_LO) * CORE + core


PLACES = [
    (y, x, z, core)
    for y in range(Y_HI * Y_LO)
    for x in range(X)
    for z in range(Z)
    for core in range(CORE)
]


def move(value, target):
    return lax.ppermute(value, AXES, [(flat(*place), flat(*target(*place))) for place in PLACES])


def y_move(value, steps):
    return move(value, lambda y, x, z, core: ((y + steps) % (Y_HI * Y_LO), x, z, core))


def x_move(value, steps):
    return move(value, lambda y, x, z, core: (y, (x + steps) % X, z, core))


def dp_move(value, flip):
    return move(value, lambda y, x, z, core: (y ^ (flip // CORE), x, z, core ^ (flip % CORE)))


YZ_GROUPS = [
    [flat(yh * Y_LO + d // CORE, x, z, d % CORE) for yh in range(Y_HI) for z in range(Z)]
    for x in range(X)
    for d in range(4)
]


def fetch_weight(weight, cut):
    half = weight.shape[0] // 2
    first = y_move(weight[:cut], 1), y_move(weight[half : half + cut], -1)
    source, first = lax.optimization_barrier((weight, first))
    return first, (y_move(source[cut:half], 1), y_move(source[half + cut :], -1))


def per_device(states, inject, final_cotangent, weight, norm_gain):
    micro_count, row_count, dim = inject.shape
    sections = lax.axis_size("section")
    section, shard = lax.axis_index("section"), lax.axis_index("dp")
    own = micro_count * row_count // sections
    place = jnp.stack([section, shard]).astype(jnp.int32)
    gain = norm_gain.reshape(1, dim)
    cut = weight.shape[0] // 84 * 16
    first, second = fetch_weight(weight, cut)

    mine = lax.all_to_all(states[0].reshape(sections, own, dim), "section", 0, 0)
    x, a, q, *a_cut = prepare(place, mine, inject, gain)

    a_ring = jnp.concatenate([a_cut[0]] + [x_move(a_cut[step], step) for step in range(1, X)])
    shared = tuple(dp_move(piece, 1) for piece in first)
    second, shared, a_ring = lax.optimization_barrier((second, shared, a_ring))
    half = weight.shape[0] // 2
    pieces, offsets = [weight, dp_move(weight, 1)], [(0, 0, 2 * half), (1, 0, 2 * half)]
    for start, piece, other in zip((0, half), first, shared):
        pieces += [piece, other]
        offsets += [(2, start, cut), (3, start, cut)]
    for start, piece in zip((cut, half + cut), second):
        pieces += [piece, dp_move(piece, 1)]
        offsets += [(2, start, half - cut), (3, start, half - cut)]
    offsets = tuple(offsets)
    a_parts = [a_ring] + [dp_move(a_ring, flip) for flip in (1, 2, 3)]

    g_parts = solve(place, pieces, offsets, a, x, q, gain, final_cotangent, TOLERANCE)

    (a_parts, g_parts) = lax.optimization_barrier((a_parts, g_parts))
    core_part, chip_part, chip_more = (dp_move(g_parts[flip], flip) for flip in (1, 2, 3))
    own_part, core_part = lax.optimization_barrier((g_parts[0], core_part))
    own_parts = [g_parts[0], x_move(own_part, 1), x_move(own_part, -1)]
    far = jnp.concatenate([core_part, chip_part, chip_more])
    far, own_parts = lax.optimization_barrier((far, own_parts))
    far_parts = [far, x_move(far, 1), x_move(far, -1)]
    own_cut, far_cut = HALVES
    halves = [
        x_move(jnp.concatenate([own_parts[1][:own_cut], far_parts[1][:far_cut]]), 1),
        x_move(jnp.concatenate([own_parts[2][own_cut:], far_parts[2][far_cut:]]), -1),
    ]
    out = block_sum(place, a_parts, halves, near_sum(place, a_parts, own_parts, far_parts))

    got = lax.all_to_all(out, AXES, 0, 0, axis_index_groups=YZ_GROUPS)
    part = dim // 64
    total = jnp.sum(got.astype(f32), axis=0)
    d_weight = total[:part]
    d_gain = total[part + 1 : part + 5].reshape(dim)
    d_inject = got[:, part, : X * own * part].reshape(Y_HI, Z, X, own, part)
    d_inject = jnp.roll(d_inject[:, :, ::-1], (section // Z) % X + 1, axis=2).transpose(0, 2, 1, 3, 4)
    d_inject = d_inject.reshape(micro_count, row_count, part).astype(f32)
    return d_inject, d_weight, d_gain


def solution(mesh):
    in_specs = (
        P("section", None, "dp", None),
        P(None, "dp", None),
        P(None, "dp", None),
        P("dp", None),
        P(),
    )
    out_specs = (P(None, "dp", "section"), P("section", "dp"), P())
    return jax.shard_map(
        per_device, mesh=mesh, in_specs=in_specs, out_specs=out_specs, check_vma=False
    )
```

```python
import functools
import math

import jax
import jax.numpy as jnp
from jax import lax
from jax.experimental import pallas as pl
from jax.experimental.pallas import tpu as pltpu
from jax.sharding import PartitionSpec as P

EPSILON = 1e-06
TOLERANCE = 2.0**-10
LANES = 128
HALVES = (64, 80, 144)
WIDE = 512
AXES = ("section", "dp")
Y_HI, X, Z, Y_LO, CORE = 2, 4, 8, 2, 2
f32, bf16 = jnp.float32, jnp.bfloat16


def own_tokens(ref, section, copies):
    block = ref[section // 4].astype(f32)
    pair = block[0:2]
    for k in range(1, 4):
        pair = jnp.where(section % 4 == k, block[2 * k : 2 * k + 2], pair)
    return jnp.concatenate([pair] * copies, axis=0)


def prepare_kernel(place_ref, states_ref, inject_ref, gain_ref, x_ref, a_ref, q_ref, *cut_refs):
    rows, dim = x_ref.shape
    section = place_ref[0]
    inject = own_tokens(inject_ref, section, 4)
    gain = gain_ref[...]
    groups = rows // 8

    def one(b, _):
        x = jnp.concatenate([states_ref[seg * groups + b].astype(f32) for seg in range(4)], axis=0) + inject
        q = lax.rsqrt(jnp.sum(x * x, axis=1, keepdims=True) * (1.0 / dim) + EPSILON)
        at = pl.ds(pl.multiple_of(b * 8, 8), 8)
        x_ref[at, :] = x
        q_ref[at, :] = jnp.broadcast_to(q, (8, LANES))
        return 0

    lax.fori_loop(0, groups, one, 0)
    a_ref[...] = (x_ref[...] * q_ref[:, 0:1] * gain).astype(bf16)
    eighth = dim // 8
    place = (section // Z) % X
    for cut_ref in cut_refs:
        cut_ref[:, 2 * eighth :] = jnp.zeros((rows, cut_ref.shape[1] - 2 * eighth), bf16)
    for own in range(X):

        @pl.when(place == own)
        def _():
            for step in range(X):
                k = (own + step) % X
                cut_refs[step][:, 0:eighth] = a_ref[:, k * eighth : (k + 1) * eighth]
                cut_refs[step][:, eighth : 2 * eighth] = a_ref[:, dim // 2 + k * eighth : dim // 2 + (k + 1) * eighth]


def prepare(place, states, inject, gain):
    rows, dim = states.shape[0] * states.shape[1], states.shape[2]
    vm = pl.BlockSpec(memory_space=pltpu.VMEM)
    return pl.pallas_call(
        prepare_kernel,
        out_shape=(
            jax.ShapeDtypeStruct((rows, dim), f32),
            jax.ShapeDtypeStruct((rows, dim), bf16),
            jax.ShapeDtypeStruct((rows, LANES), f32),
        )
        + (jax.ShapeDtypeStruct((rows, pl.cdiv(dim // 4, LANES) * LANES), bf16),) * X,
        in_specs=[pl.BlockSpec(memory_space=pltpu.SMEM)] + [vm] * 3,
        out_specs=(vm,) * (3 + X),
        compiler_params=pltpu.CompilerParams(vmem_limit_bytes=32 * 2**20),
        cost_estimate=pl.CostEstimate(flops=20 * 10**9, bytes_accessed=4 * 2**20, transcendentals=0),
    )(place, states, inject, gain)


def solve_kernel(offsets, max_sweeps, tolerance, place_ref, *refs):
    count = len(offsets)
    pieces = refs[:count]
    a_ref, x_ref, q_ref, gain_ref, final_ref = refs[count : count + 5]
    outs = refs[count + 5 : count + 9]
    w, wt, slope, t, p, v, inject_sum, gain_sum, final, sems = refs[count + 9 :]
    rows, dim = x_ref.shape
    section, shard = place_ref[0], place_ref[1]
    small, eighth, groups = dim // 4, dim // 8, rows // 8

    blocks = [(low, min(WIDE, dim - low)) for low in range(0, dim, WIDE)]
    copies = {}
    for m, (low, width) in enumerate(blocks):
        for n, ((flip, start, length), piece) in enumerate(zip(offsets, pieces)):
            at = pl.multiple_of(lax.bitwise_xor(shard, flip) * small + start, 16)
            copies[m, n] = pltpu.make_async_copy(
                piece.at[:, pl.ds(low, width)], w.at[pl.ds(at, length), pl.ds(low, width)], sems.at[m, n]
            )
            copies[m, n].start()
    final[...] = own_tokens(final_ref, section, 4)
    p[...] = jnp.zeros_like(p)
    for m, (low, width) in enumerate(blocks):
        for n in range(count):
            copies[m, n].wait()
        cols = slice(low, low + width)
        h = jnp.dot(a_ref[...], w[:, cols], preferred_element_type=f32)
        s = jax.nn.sigmoid(h)
        sl = s * (1.0 + h * (1.0 - s)) * (1.0 / math.sqrt(max_sweeps))
        slope[:, cols] = sl
        v[:, cols] = (sl * jnp.concatenate([final[:, cols]] * groups, axis=0)).astype(bf16)
        wt[cols, :] = w[:, cols].T
    sub = lax.broadcasted_iota(jnp.int32, (8, LANES), 0)

    def sweep(carry):
        done, _ = carry
        acc = jnp.zeros((rows, LANES), f32)
        for j, width in blocks:
            cols = slice(j, j + width)
            u = jnp.dot(v[...], wt[:, cols], preferred_element_type=f32)
            scaled = u * gain_ref[0:1, cols]
            t[:, cols] = scaled
            scaled = scaled * x_ref[:, cols]
            for k in range(0, width, LANES):
                acc = acc + scaled[:, k : k + LANES]
        q = q_ref[...]
        kappa = q * q * q * (jnp.sum(acc, axis=1, keepdims=True) * (1.0 / dim))

        def columns(n, sums):
            moved, size = sums
            cols = pl.ds(pl.multiple_of(n * LANES, LANES), LANES)
            run, tails = None, [None] * groups
            for b in range(groups - 1, -1, -1):
                at = slice(8 * b, 8 * b + 8)
                new = q[at] * t[at, cols] - kappa[at] * x_ref[at, cols]
                step = new - p[at, cols]
                p[at, cols] = new
                moved = moved + step * step
                run = new if run is None else run + new
                tails[b] = run
            inject_sum[:, cols] = run
            base = final[:, cols]
            for k in (2, 4, 6):
                base = base + jnp.where(sub < 8 - k, pltpu.roll(run, 8 - k, 0), 0.0)
            for b in range(groups):
                at = slice(8 * b, 8 * b + 8)
                c = base if b == groups - 1 else base + tails[b + 1]
                size = size + c * c
                v[at, cols] = (c * slope[at, cols]).astype(bf16)
            return moved, size

        zero = jnp.zeros((8, LANES), f32)
        moved, size = lax.fori_loop(0, dim // LANES, columns, (zero, zero), unroll=3)
        moved = jnp.sum(moved, axis=1, keepdims=True)
        size = jnp.sum(size, axis=1, keepdims=True)
        still = jnp.sum(jnp.where(moved <= size * (tolerance * tolerance), 0.0, 1.0))
        return done + 1, still

    lax.while_loop(
        lambda carry: jnp.logical_and(carry[0] < max_sweeps, carry[1] > 0.0),
        sweep,
        (jnp.int32(0), jnp.float32(1)),
    )

    def finish(n, _):
        cols = pl.ds(pl.multiple_of(n * LANES, LANES), LANES)
        acc = jnp.zeros((8, LANES), f32)
        for b in range(groups):
            at = slice(8 * b, 8 * b + 8)
            acc = acc + q_ref[at] * t[at, cols] * x_ref[at, cols]
        gain_sum[:, cols] = acc / gain_ref[0:1, cols]
        return 0

    lax.fori_loop(0, dim // LANES, finish, 0)
    wide_sub = lax.broadcasted_iota(jnp.int32, (8, small), 0)
    gain_rows = jnp.zeros((8, small), f32)
    total = jnp.sum(gain_sum[...], axis=0, keepdims=True)
    for k in range(4):
        gain_rows = jnp.where(wide_sub == k, total[:, k * small : (k + 1) * small], gain_rows)
    inject_rows = jnp.zeros((8, small), f32)
    total = inject_sum[...]
    total = total + pltpu.roll(total, 4, 0)
    total = total + pltpu.roll(total, 2, 0)
    for k in range(X):
        part = jnp.concatenate(
            [total[:, k * eighth : (k + 1) * eighth], total[:, dim // 2 + k * eighth : dim // 2 + (k + 1) * eighth]],
            axis=1,
        )
        inject_rows = jnp.where(wide_sub // 2 == k, part, inject_rows)
    extra = jnp.concatenate([inject_rows, gain_rows], axis=0).astype(bf16)
    for own in range(4):

        @pl.when(shard == own)
        def _():
            for flip in range(4):
                block = own ^ flip
                outs[flip][0:rows] = v[:, block * small : (block + 1) * small]

    for flip in range(4):
        outs[flip][rows : rows + 16] = extra


def solve(place, pieces, offsets, a, x, q, gain, final, tolerance):
    rows, dim = x.shape
    n = len(pieces)
    vm = pl.BlockSpec(memory_space=pltpu.VMEM)
    return pl.pallas_call(
        functools.partial(solve_kernel, offsets, 64, tolerance),
        out_shape=(jax.ShapeDtypeStruct((rows + 16, dim // 4), bf16),) * 4,
        in_specs=[pl.BlockSpec(memory_space=pltpu.SMEM)] + [pl.BlockSpec(memory_space=pl.ANY)] * n + [vm] * 5,
        out_specs=(vm,) * 4,
        scratch_shapes=[pltpu.VMEM((dim, dim), bf16)] * 2
        + [pltpu.VMEM((rows, dim), f32)] * 3
        + [pltpu.VMEM((rows, dim), bf16)]
        + [pltpu.VMEM((8, dim), f32)] * 3
        + [pltpu.SemaphoreType.DMA((pl.cdiv(dim, WIDE), n))],
        compiler_params=pltpu.CompilerParams(vmem_limit_bytes=56 * 2**20),
        cost_estimate=pl.CostEstimate(flops=4 * 10**10, bytes_accessed=16 * 2**20, transcendentals=0),
    )(place, *pieces, a, x, q, gain, final)


def own_lines(place_ref, extra):
    lines = extra[0:2]
    for k in range(1, X):
        lines = jnp.where((place_ref[0] // Z) % X == k, extra[2 * k : 2 * k + 2], lines)
    return lines


def near_kernel(rows, steps, place_ref, *refs):
    count = len(steps)
    a_refs, g_refs = refs[:4], [refs[4 + n * count : 4 + (n + 1) * count] for n in range(3)]
    block_ref, gain_ref, inject_ref, a, g, sems = refs[4 + 3 * count :]
    tall = rows + 16
    copies = [pltpu.make_async_copy(a_refs[flip], a.at[flip], sems.at[flip]) for flip in range(4)]
    for n in range(count):
        for m in range(3):
            at = g.at[pl.ds((4 * n + m) * tall, g_refs[m][n].shape[0])]
            copies.append(pltpu.make_async_copy(g_refs[m][n], at, sems.at[4 + 3 * n + m]))
    for copy in copies:
        copy.start()
    for copy in copies:
        copy.wait()
    places = [(n, step, flip) for n, step in enumerate(steps) for flip in range(4)]
    left = jnp.concatenate([a[flip, step * rows : (step + 1) * rows] for _, step, flip in places], axis=0)
    starts = [(4 * n + flip) * tall for n, _, flip in places]
    right = jnp.concatenate([g[start : start + rows] for start in starts], axis=0)
    block_ref[...] = lax.dot_general(left, right, (((0,), (0,)), ((), ())), preferred_element_type=f32)
    gain, injects = jnp.zeros(gain_ref.shape, f32), []
    for (_, _, flip), start in zip(places, starts):
        extra = g[start + rows : start + tall].astype(f32)
        gain = gain + extra[8:16]
        if flip == 0:
            injects.append(own_lines(place_ref, extra))
    gain_ref[...] = gain
    inject_ref[...] = jnp.concatenate(injects + [jnp.zeros_like(injects[0])], axis=0)


def block_kernel(rows, dim, place_ref, *refs):
    a_refs, (first, last), (near_ref, gain_ref, inject_ref) = refs[:4], refs[4:6], refs[6:9]
    out_ref, a, g, sems = refs[9:]
    small, part = dim // 4, dim // 64
    tall = rows + 16
    copies = [
        pltpu.make_async_copy(a_refs[flip].at[pl.ds(2 * rows, rows)], a.at[pl.ds(flip * rows, rows)], sems.at[flip])
        for flip in range(4)
    ]
    low = high = 0
    for n, cut in enumerate(HALVES):
        length = tall if n < 2 else 2 * tall
        one = first.at[pl.ds(low, cut)], g.at[pl.ds(n * tall, cut)]
        two = last.at[pl.ds(high, length - cut)], g.at[pl.ds(n * tall + cut, length - cut)]
        copies.append(pltpu.make_async_copy(*one, sems.at[4 + 2 * n]))
        copies.append(pltpu.make_async_copy(*two, sems.at[5 + 2 * n]))
        low, high = low + cut, high + length - cut
    for copy in copies:
        copy.start()
    for copy in copies:
        copy.wait()
    right = jnp.concatenate([g[flip * tall : flip * tall + rows] for flip in range(4)], axis=0)
    block = lax.dot_general(a[...], right, (((0,), (0,)), ((), ())), preferred_element_type=f32) + near_ref[...]
    extras = [g[flip * tall + rows : (flip + 1) * tall].astype(f32) for flip in range(4)]
    gain = gain_ref[...] + extras[0][8:16] + extras[1][8:16] + extras[2][8:16] + extras[3][8:16]
    inject = inject_ref[...]
    inject = jnp.concatenate([inject[0:4], own_lines(place_ref, extras[0]), inject[4:6]], axis=0)
    for k in range(16):
        line = jnp.concatenate(
            [inject[n : n + 1, k * part : (k + 1) * part] for n in range(8)] + [jnp.zeros((1, small - 8 * part), f32)],
            axis=1,
        )
        out_ref[k] = jnp.concatenate([block[k * part : (k + 1) * part], line, gain[0:5]], axis=0).astype(bf16)


def near_sum(place, a_parts, own_parts, core_parts, chip_parts):
    steps = (0, 1, 3)
    (deep, wide), (tall, small) = a_parts[0].shape, own_parts[0].shape
    hold, vm = pl.BlockSpec(memory_space=pl.ANY), pl.BlockSpec(memory_space=pltpu.VMEM)
    return pl.pallas_call(
        functools.partial(near_kernel, deep // X, steps),
        out_shape=(
            jax.ShapeDtypeStruct((wide, small), f32),
            jax.ShapeDtypeStruct((8, small), f32),
            jax.ShapeDtypeStruct((8, small), f32),
        ),
        in_specs=[pl.BlockSpec(memory_space=pltpu.SMEM)] + [hold] * 13,
        out_specs=(vm,) * 3,
        scratch_shapes=[
            pltpu.VMEM((4, deep, wide), bf16),
            pltpu.VMEM((12 * tall, small), bf16),
            pltpu.SemaphoreType.DMA((13,)),
        ],
        compiler_params=pltpu.CompilerParams(vmem_limit_bytes=40 * 2**20),
        cost_estimate=pl.CostEstimate(flops=5 * 10**9, bytes_accessed=6 * 2**20, transcendentals=0),
    )(place, *a_parts, *own_parts, *core_parts, *chip_parts)


def block_sum(place, a_parts, halves, near):
    (deep, wide), small = a_parts[0].shape, halves[0].shape[1]
    rows = deep // X
    hold, vm = pl.BlockSpec(memory_space=pl.ANY), pl.BlockSpec(memory_space=pltpu.VMEM)
    return pl.pallas_call(
        functools.partial(block_kernel, rows, 4 * small),
        out_shape=jax.ShapeDtypeStruct((16, 48, small), bf16),
        in_specs=[pl.BlockSpec(memory_space=pltpu.SMEM)] + [hold] * 6 + [vm] * 3,
        out_specs=vm,
        scratch_shapes=[
            pltpu.VMEM((4 * rows, wide), bf16),
            pltpu.VMEM((4 * (rows + 16), small), bf16),
            pltpu.SemaphoreType.DMA((10,)),
        ],
        compiler_params=pltpu.CompilerParams(vmem_limit_bytes=40 * 2**20),
    )(place, *a_parts, *halves, *near)


def flat(y, x, z, core):
    return (((y // Y_LO) * X + x) * Z + z) * 4 + (y % Y_LO) * CORE + core


PLACES = [
    (y, x, z, core)
    for y in range(Y_HI * Y_LO)
    for x in range(X)
    for z in range(Z)
    for core in range(CORE)
]


def move(value, target):
    return lax.ppermute(value, AXES, [(flat(*place), flat(*target(*place))) for place in PLACES])


def y_move(value, steps):
    return move(value, lambda y, x, z, core: ((y + steps) % (Y_HI * Y_LO), x, z, core))


def x_move(value, steps):
    return move(value, lambda y, x, z, core: (y, (x + steps) % X, z, core))


def dp_move(value, flip):
    return move(value, lambda y, x, z, core: (y ^ (flip // CORE), x, z, core ^ (flip % CORE)))


YZ_GROUPS = [
    [flat(yh * Y_LO + d // CORE, x, z, d % CORE) for yh in range(Y_HI) for z in range(Z)]
    for x in range(X)
    for d in range(4)
]


def fetch_weight(weight, cut):
    half = weight.shape[0] // 2
    first = y_move(weight[:cut], 1), y_move(weight[half : half + cut], -1)
    source, first = lax.optimization_barrier((weight, first))
    return first, (y_move(source[cut:half], 1), y_move(source[half + cut :], -1))


def per_device(states, inject, final_cotangent, weight, norm_gain):
    micro_count, row_count, dim = inject.shape
    sections = lax.axis_size("section")
    section, shard = lax.axis_index("section"), lax.axis_index("dp")
    own = micro_count * row_count // sections
    place = jnp.stack([section, shard]).astype(jnp.int32)
    gain = norm_gain.reshape(1, dim)
    cut = weight.shape[0] // 84 * 16
    first, second = fetch_weight(weight, cut)

    mine = lax.all_to_all(states[0].reshape(sections, own, dim), "section", 0, 0)
    x, a, q, *a_cut = prepare(place, mine, inject, gain)

    a_ring = jnp.concatenate([a_cut[0]] + [x_move(a_cut[step], step) for step in range(1, X)])
    shared = tuple(dp_move(piece, 1) for piece in first)
    second, shared, a_ring = lax.optimization_barrier((second, shared, a_ring))
    half = weight.shape[0] // 2
    pieces, offsets = [weight, dp_move(weight, 1)], [(0, 0, 2 * half), (1, 0, 2 * half)]
    for start, piece, other in zip((0, half), first, shared):
        pieces += [piece, other]
        offsets += [(2, start, cut), (3, start, cut)]
    for start, piece in zip((cut, half + cut), second):
        pieces += [piece, dp_move(piece, 1)]
        offsets += [(2, start, half - cut), (3, start, half - cut)]
    offsets = tuple(offsets)
    a_parts = [a_ring] + [dp_move(a_ring, flip) for flip in (1, 2, 3)]

    g_parts = solve(place, pieces, offsets, a, x, q, gain, final_cotangent, TOLERANCE)

    (a_parts, g_parts) = lax.optimization_barrier((a_parts, g_parts))
    core_part, chip_part, chip_more = (dp_move(g_parts[flip], flip) for flip in (1, 2, 3))
    own_part, core_part = lax.optimization_barrier((g_parts[0], core_part))
    own_parts = [g_parts[0], x_move(own_part, 1), x_move(own_part, -1)]
    core_parts = [core_part, x_move(core_part, 1), x_move(core_part, -1)]
    chip = jnp.concatenate([chip_part, chip_more])
    chip, own_parts, core_parts = lax.optimization_barrier((chip, own_parts, core_parts))
    chip_parts = [chip, x_move(chip, 1), x_move(chip, -1)]
    groups = tuple(zip(HALVES, (own_parts, core_parts, chip_parts)))
    halves = [
        x_move(jnp.concatenate([parts[1][:cut] for cut, parts in groups]), 1),
        x_move(jnp.concatenate([parts[2][cut:] for cut, parts in groups]), -1),
    ]
    near = near_sum(place, a_parts, own_parts, core_parts, chip_parts)
    out = block_sum(place, a_parts, halves, near)

    got = lax.all_to_all(out, AXES, 0, 0, axis_index_groups=YZ_GROUPS)
    part = dim // 64
    total = jnp.sum(got.astype(f32), axis=0)
    d_weight = total[:part]
    d_gain = total[part + 1 : part + 5].reshape(dim)
    d_inject = got[:, part, : X * own * part].reshape(Y_HI, Z, X, own, part)
    d_inject = jnp.roll(d_inject[:, :, ::-1], (section // Z) % X + 1, axis=2).transpose(0, 2, 1, 3, 4)
    d_inject = d_inject.reshape(micro_count, row_count, part).astype(f32)
    return d_inject, d_weight, d_gain


def solution(mesh):
    in_specs = (
        P("section", None, "dp", None),
        P(None, "dp", None),
        P(None, "dp", None),
        P("dp", None),
        P(),
    )
    out_specs = (P(None, "dp", "section"), P("section", "dp"), P())
    return jax.shard_map(
        per_device, mesh=mesh, in_specs=in_specs, out_specs=out_specs, check_vma=False
    )
```
